32 devices in a mesh: dp: 16 (over z, x, core), tensor: 2 (over y).
Axes of the slice: x: 2, y: 2, z: 4, core: 2. Of those that a mesh axis runs over, the one named last changes fastest.
Arguments:
- text_rows: bfloat16 [32, 512, 768], P('dp'), may hold values from -6 to 6
- vision_rows: bfloat16 [32, 256, 768], P('dp'), may hold values from -6 to 6
- segment_ids: int32 [32, 512], P('dp'), may hold values from 0 to 63, never falling along the last dimension, each value on 1 to 256 neighbouring positions
- text_keep: int32 [32, 512], P('dp'), may hold values 0 or 1
- segment_box: int32 [32, 64, 2], P('dp'), may hold values from 0 to 15
- patch_keep: int32 [32, 256], P('dp'), may hold values 0 or 1
- attn_qkv_a: bfloat16 [768, 3, 768], P('dp', None, 'tensor'), may hold values from -0.21875 to 0.21875
- attn_out_a: bfloat16 [768, 768], P('tensor', 'dp'), may hold values from -1.75 to 1.75
- mlp_in_a: bfloat16 [768, 3072], P('dp', 'tensor'), may hold values from -0.21875 to 0.21875
- mlp_out_a: bfloat16 [3072, 768], P('tensor', 'dp'), may hold values from -0.109375 to 0.109375
- norm_gain_a: bfloat16 [2, 768], P(None, 'dp'), may hold values from 0.5 to 1.5
- norm_shift_a: bfloat16 [2, 768], P(None, 'dp'), may hold values from -4 to 4
- box_table_a: bfloat16 [12, 2, 31], P('tensor'), may hold values from -6 to 6
- attn_query_b: bfloat16 [768, 768], P('dp', 'tensor'), may hold values from -0.21875 to 0.21875
- attn_kv_b: bfloat16 [768, 2, 768], P('dp', None, 'tensor'), may hold values from -0.21875 to 0.21875
- attn_out_b: bfloat16 [768, 768], P('tensor', 'dp'), may hold values from -1.75 to 1.75
- mlp_in_b: bfloat16 [768, 3072], P('dp', 'tensor'), may hold values from -0.21875 to 0.21875
- mlp_out_b: bfloat16 [3072, 768], P('tensor', 'dp'), may hold values from -0.109375 to 0.109375
- norm_gain_b: bfloat16 [2, 768], P(None, 'dp'), may hold values from 0.5 to 1.5
- norm_shift_b: bfloat16 [2, 768], P(None, 'dp'), may hold values from -4 to 4
- box_table_b: bfloat16 [12, 2, 31], P('tensor'), may hold values from -6 to 6
- out_grad: bfloat16 [32, 512, 768], P('dp', 'tensor'), may hold values from -6 to 6
Outputs:
- layer_out: bfloat16 [32, 512, 768], P('dp', 'tensor')
- text_grad: float32 [32, 512, 768], P('dp', 'tensor')
- vision_grad: float32 [32, 256, 768], P('dp', 'tensor')
- grad_qkv_a: float32 [768, 3, 768], P('dp', None, 'tensor')
- grad_out_a: float32 [768, 768], P('tensor', 'dp')
- grad_in_a: float32 [768, 3072], P('dp', 'tensor')
- grad_mlp_a: float32 [3072, 768], P('tensor', 'dp')
- grad_gain_a: float32 [2, 768], P(None, 'dp')
- grad_shift_a: float32 [2, 768], P(None, 'dp')
- grad_table_a: float32 [12, 2, 31], P('tensor')
- grad_query_b: float32 [768, 768], P('dp', 'tensor')
- grad_kv_b: float32 [768, 2, 768], P('dp', None, 'tensor')
- grad_out_b: float32 [768, 768], P('tensor', 'dp')
- grad_in_b: float32 [768, 3072], P('dp', 'tensor')
- grad_mlp_b: float32 [3072, 768], P('tensor', 'dp')
- grad_gain_b: float32 [2, 768], P(None, 'dp')
- grad_shift_b: float32 [2, 768], P(None, 'dp')
- grad_table_b: float32 [12, 2, 31], P('tensor')
The draws below stay inside these ranges and needn't reach their ends.
Inputs may be any that keep to these rules, and one draw needn't show every extreme that they name: `segment_ids`: each page's segment numbers never fall, every one of the 64 segments has a token, and one segment holds 512 // 2 tokens.
All inputs are finite; a program needn't handle non-finite values. No bound on the sum of `text_keep` or of `patch_keep` on one device may be relied on, other than what follows from the above.
Results may differ from the reference program's by a relative error of at most 0.025.
Values may be sent and summed in bfloat16 or wider, within the bound.
No kernel may reach another device: no remote copies, remote signals or barrier semaphores. Data moves between devices by JAX's collectives and lax.ppermute only.
A program may use at most 192 MiB of HBM per device.

```python
import math
import jax
import jax.numpy as jnp
import numpy as np
from jax import lax

D = 768
HEADS = 12
HD = 64
FF = 3072
LEN = 512
GRID = 16
VIS = 256
RELS = 31
SEGS = 64
PAGES = 32


def plant(values, stream_key, low, top_value):
    extent = values.shape
    spot = [jax.random.randint(jax.random.fold_in(stream_key, axis), (), 0, extent[axis]) for axis in range(len(extent))]
    values = values.at[tuple(spot)].set(low)
    longest = extent.index(max(extent))
    spot[longest] = (spot[longest] + 1) % extent[longest]
    return values.at[tuple(spot)].set(top_value)


def steps_of(rng, extent, cuts, smallest, largest):
    level, own = 1.0, jax.random.fold_in(rng, 6)
    for position, parts in cuts:
        heights = jnp.exp(jax.random.uniform(jax.random.fold_in(own, position), (parts,), jnp.float32, smallest / len(cuts), largest / len(cuts)))
        level = level * jnp.repeat(heights, extent[position] // parts).reshape([-1 if axis == position else 1 for axis in range(len(extent))])
    return level


def length_profile(amount, total, bound, skew):
    portions = [(1 << 20) // math.isqrt(rank ** skew) + 1 for rank in range(2, amount + 1)]
    spare, given = total - bound - (amount - 1), [1] * (amount - 1)
    while spare > 0:
        free = [i for i in range(amount - 1) if given[i] < bound]
        pool, remaining = sum([portions[i] for i in free]), spare
        for i in free:
            more = min(bound - given[i], max(1, remaining * portions[i] // pool), spare)
            given[i] = given[i] + more
            spare = spare - more
    return np.array([bound] + given)


def ragged_sizes(own_key, amount, total, limit, skew):
    if amount == 2:
        one = jax.random.randint(own_key, (), max(1, total - limit), min(limit, total - 1) + 1)
        return jnp.stack([one, total - one])
    lengths = jnp.asarray(length_profile(amount, total, limit, skew), jnp.int32)
    twos = (amount - 1) // 2
    source_of, taker = lengths[1:1 + 2 * twos:2], lengths[2:2 + 2 * twos:2]
    margin = jnp.minimum(source_of - 1, limit - taker)
    shifted = jax.random.randint(jax.random.fold_in(own_key, 1), (twos,), 0, 1 << 20) % (margin + 1)
    lengths = lengths.at[1:1 + 2 * twos:2].set(source_of - shifted).at[2:2 + 2 * twos:2].set(taker + shifted)
    return lengths[jax.random.permutation(jax.random.fold_in(own_key, 2), amount)]


def normal_values(stream_key, extent, scale, most, split=(), kind=jnp.bfloat16):
    entries = scale * jax.random.normal(stream_key, extent, jnp.float32)
    if split:
        entries = entries * steps_of(stream_key, extent, split, -0.22, 0.18)
    return jnp.clip(entries, -most, most).astype(kind)


def setup_inputs(seed: int = 0) -> dict:
    keys = jax.random.split(jax.random.key(seed), 23)
    return {
        "text_rows": normal_values(keys[0], (PAGES, LEN, D), 1.0, 6.0, ((0, 16),)),
        "vision_rows": normal_values(keys[1], (PAGES, VIS, D), 1.0, 6.0, ((0, 16),)),
        "segment_ids": jax.vmap(lambda own: jnp.searchsorted(jnp.cumsum(ragged_sizes(own, SEGS, LEN, LEN // 2, 2)), jnp.arange(LEN), side="right"))(jax.random.split(keys[2], PAGES)).reshape((PAGES, LEN)).astype(jnp.int32),
        "text_keep": plant((jax.random.randint(keys[3], (PAGES, LEN), 0, 8) < 7).astype(jnp.int32), jax.random.fold_in(keys[3], 1), 0, 1),
        "segment_box": plant(jax.random.randint(keys[4], (PAGES, SEGS, 2), 0, GRID), jax.random.fold_in(keys[4], 1), 0, GRID - 1).astype(jnp.int32),
        "patch_keep": plant((jax.random.randint(keys[5], (PAGES, VIS), 0, 4) < 3).astype(jnp.int32), jax.random.fold_in(keys[5], 1), 0, 1),
        "attn_qkv_a": normal_values(keys[6], (D, 3, D), D ** -0.5, 0.21875, ((0, 16), (2, 2))),
        "attn_out_a": normal_values(keys[7], (D, D), (max(D // 64, 1)) ** -0.5, 1.75, ((0, 2), (1, 16))),
        "mlp_in_a": normal_values(keys[8], (D, FF), D ** -0.5, 0.21875, ((0, 16), (1, 2))),
        "mlp_out_a": normal_values(keys[9], (FF, D), FF ** -0.5, 0.109375, ((0, 2), (1, 16))),
        "norm_gain_a": jnp.clip(1.0 + 0.1 * jax.random.normal(keys[10], (2, D), jnp.float32), 0.5, 1.5).astype(jnp.bfloat16),
        "norm_shift_a": normal_values(keys[11], (2, D), 0.3, 4.0, ((1, 16),)),
        "box_table_a": normal_values(keys[12], (HEADS, 2, RELS), 0.5, 6.0, ((0, 2),)),
        "attn_query_b": normal_values(keys[13], (D, D), D ** -0.5, 0.21875, ((0, 16), (1, 2))),
        "attn_kv_b": normal_values(keys[14], (D, 2, D), D ** -0.5, 0.21875, ((0, 16), (2, 2))),
        "attn_out_b": normal_values(keys[15], (D, D), (max(D // 64, 1)) ** -0.5, 1.75, ((0, 2), (1, 16))),
        "mlp_in_b": normal_values(keys[16], (D, FF), D ** -0.5, 0.21875, ((0, 16), (1, 2))),
        "mlp_out_b": normal_values(keys[17], (FF, D), FF ** -0.5, 0.109375, ((0, 2), (1, 16))),
        "norm_gain_b": jnp.clip(1.0 + 0.1 * jax.random.normal(keys[18], (2, D), jnp.float32), 0.5, 1.5).astype(jnp.bfloat16),
        "norm_shift_b": normal_values(keys[19], (2, D), 0.3, 4.0, ((1, 16),)),
        "box_table_b": normal_values(keys[20], (HEADS, 2, RELS), 0.5, 6.0, ((0, 2),)),
        "out_grad": normal_values(keys[21], (PAGES, LEN, D), 1.0, 6.0, ((0, 16), (1, 2))),
    }


highest = lax.Precision.HIGHEST
epsilon = 1e-06
masked_score = -30000.0

@jax.custom_vjp
def low(v):
    return lax.optimization_barrier(v.astype(jnp.bfloat16)).astype(jnp.float32)

@jax.custom_vjp
def low_back(v):
    return v

def low_keep(v):
    return (low(v), None)

def low_pass(kept, grad):
    return (grad,)

def back_keep(v):
    return (v, None)

def back_low(kept, grad):
    return (low(grad),)
low.defvjp(low_keep, low_pass)
low_back.defvjp(back_keep, back_low)

def matmul(left_side, right_side):
    return jnp.dot(left_side, right_side, precision=highest)

def norm_rows(values, norm_gain, norm_shift):
    center = values - lax.optimization_barrier(jnp.mean(values, axis=-1, keepdims=True))
    spread = lax.optimization_barrier(jnp.mean(center * center, axis=-1, keepdims=True))
    return center * lax.rsqrt(spread + epsilon) * norm_gain + norm_shift

def box_bias(bias_table, row_x, row_y, col_x, col_y):
    rel_x = row_x[:, None] - col_x[None, :] + (GRID - 1)
    rel_y = row_y[:, None] - col_y[None, :] + (GRID - 1)
    return bias_table[:, 0][:, rel_x] + bias_table[:, 1][:, rel_y]

def attend(queries, key_rows, values, page_bias, key_keep):
    scores = jnp.einsum('qhd,khd->hqk', queries, key_rows, precision=highest) * HD ** (-0.5) + page_bias
    scores = low_back(jnp.where(key_keep[None, None, :] > 0, scores, masked_score))
    attn_probs = low(jax.nn.softmax(scores, axis=-1))
    return jnp.einsum('hqk,khd->qhd', attn_probs, values, precision=highest)

def forward(text_rows, vision_rows, attn_qkv_a, attn_out_a, mlp_in_a, mlp_out_a, norm_gain_a, norm_shift_a, box_table_a, attn_query_b, attn_kv_b, attn_out_b, mlp_in_b, mlp_out_b, norm_gain_b, norm_shift_b, box_table_b, token_box, text_keep, patch_keep):
    page_count = text_rows.shape[0]
    rows_text = text_rows.reshape(-1, D)
    rows_vision = vision_rows.reshape(-1, D)
    mix_qkv = low_back(low(matmul(rows_text, attn_qkv_a.reshape(D, 3 * D))))
    mix_qkv = mix_qkv.reshape(page_count, LEN, 3, HEADS, HD)

    def self_page(page_item):
        queries, key_rows, values, page_box, key_keep = page_item
        page_bias = box_bias(box_table_a, page_box[:, 0], page_box[:, 1], page_box[:, 0], page_box[:, 1])
        return attend(queries, key_rows, values, page_bias, key_keep)
    context_a = lax.map(jax.checkpoint(self_page), (mix_qkv[:, :, 0], mix_qkv[:, :, 1], mix_qkv[:, :, 2], token_box, text_keep))
    context_a = low_back(low(context_a.reshape(-1, D)))
    mixed_a = norm_rows(rows_text + low_back(matmul(context_a, attn_out_a)), norm_gain_a[0], norm_shift_a[0])
    hidden_a = low_back(matmul(low(mixed_a), mlp_in_a))
    branch_a = low_back(matmul(low(jax.nn.gelu(hidden_a, approximate=False)), mlp_out_a))
    middle = norm_rows(mixed_a + branch_a, norm_gain_a[1], norm_shift_a[1])
    queries_b = low_back(low(matmul(low(middle), attn_query_b))).reshape(page_count, LEN, HEADS, HD)
    mix_kv = low_back(low(matmul(rows_vision, attn_kv_b.reshape(D, 2 * D)))).reshape(page_count, VIS, 2, HEADS, HD)
    grid_index = jnp.arange(VIS, dtype=jnp.int32)
    patch_x = grid_index % GRID
    patch_y = grid_index // GRID

    def cross_page(page_item):
        queries, key_rows, values, page_box, key_keep = page_item
        page_bias = box_bias(box_table_b, page_box[:, 0], page_box[:, 1], patch_x, patch_y)
        return attend(queries, key_rows, values, page_bias, key_keep)
    context_b = lax.map(jax.checkpoint(cross_page), (queries_b, mix_kv[:, :, 0], mix_kv[:, :, 1], token_box, patch_keep))
    context_b = low_back(low(context_b.reshape(-1, D)))
    mixed_b = norm_rows(middle + low_back(matmul(context_b, attn_out_b)), norm_gain_b[0], norm_shift_b[0])
    hidden_b = low_back(matmul(low(mixed_b), mlp_in_b))
    branch_b = low_back(matmul(low(jax.nn.gelu(hidden_b, approximate=False)), mlp_out_b))
    final_rows = norm_rows(mixed_b + branch_b, norm_gain_b[1], norm_shift_b[1])
    return final_rows.reshape(page_count, LEN, D)

def reference(text_rows, vision_rows, segment_ids, text_keep, segment_box, patch_keep, attn_qkv_a, attn_out_a, mlp_in_a, mlp_out_a, norm_gain_a, norm_shift_a, box_table_a, attn_query_b, attn_kv_b, attn_out_b, mlp_in_b, mlp_out_b, norm_gain_b, norm_shift_b, box_table_b, out_grad):
    token_box = jax.vmap(lambda page_box, page_ids: page_box[page_ids])(segment_box, segment_ids)
    floats = (text_rows, vision_rows, attn_qkv_a, attn_out_a, mlp_in_a, mlp_out_a, norm_gain_a, norm_shift_a, box_table_a, attn_query_b, attn_kv_b, attn_out_b, mlp_in_b, mlp_out_b, norm_gain_b, norm_shift_b, box_table_b)
    floats = tuple((array_part.astype(jnp.float32) for array_part in floats))

    def run_layers(*weights_all):
        return forward(*weights_all, token_box, text_keep, patch_keep)
    result, pull_back = jax.vjp(run_layers, *floats)
    all_grads = pull_back(out_grad.astype(jnp.float32))
    return (result.astype(jnp.bfloat16), all_grads[0], all_grads[1], all_grads[2], all_grads[3], all_grads[4], all_grads[5], all_grads[6], all_grads[7], all_grads[8], all_grads[9], all_grads[10], all_grads[11], all_grads[12], all_grads[13], all_grads[14], all_grads[15], all_grads[16])
```

```python
import jax
import jax.numpy as jnp
from jax import lax
from jax.sharding import PartitionSpec as P

HD = 64
GRID = 16
RELS = 2 * GRID - 1
LANES = 128

highest = lax.Precision.HIGHEST
epsilon = 1e-06
masked_score = -30000.0
bf16 = jnp.bfloat16
f32 = jnp.float32


def cast_low(values):
    return values.astype(bf16)


def matmul(left_side, right_side):
    return jnp.dot(left_side, right_side, preferred_element_type=f32)


def matmul_tn(left_side, right_side):
    return lax.dot_general(
        left_side, right_side, (((0,), (0,)), ((), ())), preferred_element_type=f32
    )


def matmul_nt(left_side, right_side):
    return lax.dot_general(
        left_side, right_side, (((1,), (1,)), ((), ())), preferred_element_type=f32
    )


def norm_forward(values, gain, shift):
    center = values - jnp.mean(values, axis=-1, keepdims=True)
    scale = lax.rsqrt(jnp.mean(center * center, axis=-1, keepdims=True) + epsilon)
    normed = center * scale
    return normed * gain + shift, normed, scale


def norm_backward(grad, normed, scale, gain):
    scaled = grad * gain
    inner = scaled - jnp.mean(scaled, axis=-1, keepdims=True)
    inner = inner - normed * jnp.mean(scaled * normed, axis=-1, keepdims=True)
    return inner * scale, jnp.sum(grad * normed, axis=0), jnp.sum(grad, axis=0)


def gelu_pair(hidden):
    cdf = 0.5 * lax.erfc(-hidden * (0.5**0.5))
    slope = cdf + hidden * jnp.exp(-0.5 * hidden * hidden) * (0.3989422804014327)
    return cast_low(hidden * cdf), cast_low(slope)


def grid_hot(coords):
    hot = coords[:, :, None] == jnp.arange(GRID, dtype=jnp.int32)
    return hot.reshape(coords.shape[0], 2 * GRID)


def pair_tables(tables):
    offset = jnp.arange(GRID)[:, None] - jnp.arange(GRID)[None, :] + GRID - 1
    hot = (offset[:, :, None] == jnp.arange(RELS)).astype(f32)
    pairs = jnp.einsum("hcr,abr->cahb", tables.astype(f32), hot, precision=highest)
    same = jnp.eye(2, dtype=f32)
    spread = pairs[:, :, :, None, :] * same[:, None, None, :, None]
    return cast_low(spread.reshape(2 * GRID, -1))


def table_grad(own_hot, right_part):
    heads = right_part.shape[0]
    pairs = jnp.einsum(
        "na,hnb->hab", own_hot.astype(f32), right_part, precision=highest
    ).reshape(heads, 2, GRID, 2, GRID)
    pairs = jnp.stack([pairs[:, 0, :, 0], pairs[:, 1, :, 1]], axis=1)
    offset = jnp.arange(GRID)[:, None] - jnp.arange(GRID)[None, :] + GRID - 1
    hot = (offset[:, :, None] == jnp.arange(RELS)).astype(f32)
    return jnp.einsum("hcab,abr->hcr", pairs, hot, precision=highest)


def split_heads(rows):
    return jnp.transpose(rows.reshape(rows.shape[0], -1, HD), (1, 0, 2))


def merge_heads(heads):
    return jnp.transpose(heads, (1, 0, 2)).reshape(heads.shape[1], -1)


def scores_of(queries, keys, own_part, other_hot, keep):
    scores = jnp.einsum("hqd,hkd->hqk", queries, keys, preferred_element_type=f32) * HD**-0.5
    scores = scores + jnp.einsum("hqb,kb->hqk", own_part, other_hot, preferred_element_type=f32)
    return jnp.where(keep[None, None, :] > 0, scores, masked_score)


def attend_forward(queries, keys, values, own_part, other_hot, keep):
    scores = scores_of(split_heads(queries), split_heads(keys), own_part, other_hot, keep)
    top = jnp.max(scores, axis=-1, keepdims=True)
    weights = jnp.exp(scores - top)
    total = jnp.sum(weights, axis=-1, keepdims=True)
    probs = cast_low(weights / total)
    context = jnp.einsum("hqk,hkd->hqd", probs, split_heads(values), preferred_element_type=f32)
    return merge_heads(cast_low(context)), top + jnp.log(total)


def attend_backward(queries, keys, values, own_part, other_hot, keep, log_total, context_grad):
    queries, keys, values = split_heads(queries), split_heads(keys), split_heads(values)
    context_grad = split_heads(context_grad)
    scores = scores_of(queries, keys, own_part, other_hot, keep)
    probs = jnp.exp(scores - log_total)
    prob_grad = jnp.einsum("hqd,hkd->hqk", context_grad, values, preferred_element_type=f32)
    row_dot = jnp.sum(probs * prob_grad, axis=-1, keepdims=True)
    score_grad = cast_low(probs * (prob_grad - row_dot) * (keep[None, None, :] > 0))
    query_grad = jnp.einsum("hqk,hkd->hqd", score_grad, keys, preferred_element_type=f32)
    key_grad = jnp.einsum("hqk,hqd->hkd", score_grad, queries, preferred_element_type=f32)
    value_grad = jnp.einsum(
        "hqk,hqd->hkd", cast_low(probs), context_grad, preferred_element_type=f32
    )
    right_part = jnp.einsum("hqk,kb->hqb", score_grad, other_hot, preferred_element_type=f32)
    return (
        merge_heads(cast_low(query_grad * HD**-0.5)),
        merge_heads(cast_low(key_grad * HD**-0.5)),
        merge_heads(cast_low(value_grad)),
        right_part,
    )


def shards(
    text_rows,
    vision_rows,
    segment_ids,
    text_keep,
    segment_box,
    patch_keep,
    attn_qkv_a,
    attn_out_a,
    mlp_in_a,
    mlp_out_a,
    norm_gain_a,
    norm_shift_a,
    box_table_a,
    attn_query_b,
    attn_kv_b,
    attn_out_b,
    mlp_in_b,
    mlp_out_b,
    norm_gain_b,
    norm_shift_b,
    box_table_b,
    out_grad,
):
    pages, length, width = text_rows.shape
    patches = vision_rows.shape[1]
    ndp, nt = lax.axis_size("dp"), lax.axis_size("tensor")
    own, mine = lax.axis_index("dp"), lax.axis_index("tensor")
    block = width // ndp
    share = attn_out_a.shape[0]
    hidden = mlp_in_a.shape[1]
    nz = ndp // 4
    copies = nt // pages

    def swap(values, dp_mask, tensor_mask):
        pairs = [
            (d * nt + t, (d ^ dp_mask) * nt + (t ^ tensor_mask))
            for d in range(ndp)
            for t in range(nt)
        ]
        return lax.ppermute(values, ("dp", "tensor"), pairs)

    def in_order(relative):
        return [
            lax.select_n(mine, *[relative[a ^ m] for m in range(nt)])
            for a in range(nt)
        ]

    def gather_rows(piece):
        slab = jnp.concatenate([piece] + [swap(piece, 4 * k, 0) for k in range(1, nz)], axis=0)
        if nt == 2:
            half = slab.shape[0] // 2
            along_x, along_y = swap(slab, 2, 0), swap(slab, 0, 1)
            far = jnp.concatenate(
                [swap(along_y[:half], 2, 0), swap(along_x[half:], 0, 1)], axis=0
            )
            plane = [[slab, along_x], [along_y, far]]
        else:
            pair = [slab, swap(slab, 2, 0)]
            plane = [pair] + [[swap(p, 0, j) for p in pair] for j in range(1, nt)]
        whole = []
        for pair in plane:
            rows = jnp.concatenate(pair, axis=0)
            whole.append(jnp.concatenate([rows, swap(rows, 1, 0)], axis=0))
        return whole

    def columns(whole, start, size):
        return jnp.concatenate([rows[:, start : start + size] for rows in whole], axis=1)

    def scatter_rows(products, groups):
        high = width // 2
        sums = []
        for left_side, right_side in products:
            away = cast_low(matmul_tn(left_side[:, high:], right_side) * (1.0 / copies))
            sums.append(
                cast_low(
                    matmul_tn(left_side[:, :high], right_side) * (1.0 / copies)
                    + swap(away, 1, 0).astype(f32)
                )
            )
        rows = high // 2

        def part(x, j):
            out = []
            for total, count in zip(sums, groups):
                size = total.shape[1] // count
                own_size = size // nt
                for g in range(count):
                    start = g * size + j * own_size
                    out.append(total[x * rows : (x + 1) * rows, start : start + own_size])
            return jnp.concatenate(out, axis=1) if len(out) > 1 else out[0]

        if nt == 2:
            half = rows // 2
            far, near_x, near_y, here = part(1, 1), part(1, 0), part(0, 1), part(0, 0)
            from_x, from_y = swap(far[:half], 2, 0), swap(far[half:], 0, 1)
            near_y = jnp.concatenate([near_y[:half] + from_x, near_y[half:]], axis=0)
            near_x = jnp.concatenate([near_x[:half], near_x[half:] + from_y], axis=0)
            here = here.astype(f32) + swap(near_x, 2, 0) + swap(near_y, 0, 1)
        else:
            here = [part(0, j) + swap(part(1, j), 2, 0) for j in range(nt)]
            here = here[0].astype(f32) + sum(swap(here[j], 0, j).astype(f32) for j in range(1, nt))
        here = cast_low(here)
        out = here[:block].astype(f32)
        for k in range(1, nz):
            out = out + swap(here[k * block : (k + 1) * block], 4 * k, 0).astype(f32)
        return out

    def sum_all(values):
        total = values[0]
        for j in range(1, nt):
            total = total + swap(values[j], 0, j)
        for mask in (1, 2):
            total = total + swap(total, mask, 0)
        return sum([swap(total, 4 * k, 0) for k in range(1, nz)], total)

    def to_owners(rows):
        cut = rows.shape[0] // nt
        parts = [rows[a * cut : (a + 1) * cut] for a in range(nt)]
        relative = in_order(parts)
        arrived = [relative[0]] + [swap(relative[k], 0, k) for k in range(1, nt)]
        return jnp.stack(in_order(arrived)[::copies])

    def from_owners(shares):
        relative = in_order([shares[a // copies] for a in range(nt)])
        arrived = [relative[0]] + [swap(relative[k], 0, k) for k in range(1, nt)]
        return jnp.concatenate(in_order(arrived), axis=0)

    norms = jnp.concatenate([norm_gain_a, norm_shift_a, norm_gain_b, norm_shift_b], axis=0)
    norm_columns = jnp.pad(norms.T, ((0, 0), (0, LANES - norms.shape[0])))
    first = gather_rows(
        jnp.concatenate([attn_qkv_a.reshape(block, 3 * share), attn_out_a.T, norm_columns], axis=1)
    )
    in_a = gather_rows(mlp_in_a)
    back_a = gather_rows(mlp_out_a.T)
    second = gather_rows(
        jnp.concatenate([attn_query_b, attn_kv_b.reshape(block, 2 * share), attn_out_b.T], axis=1)
    )
    in_b = gather_rows(mlp_in_b)
    back_b = gather_rows(mlp_out_b.T)
    qkv_a = jnp.concatenate([columns(first, i * share, share) for i in range(3)], axis=1)
    out_a = columns(first, 3 * share, share)
    norms = first[0][:, 4 * share : 4 * share + 8].T.astype(f32)
    gains, shifts = [norms[0], norms[1], norms[4], norms[5]], [norms[2], norms[3], norms[6], norms[7]]
    query_b = columns(second, 0, share)
    kv_b = jnp.concatenate([columns(second, share, share), columns(second, 2 * share, share)], axis=1)
    out_b = columns(second, 3 * share, share)
    in_a, back_a = columns(in_a, 0, hidden), columns(back_a, 0, hidden)
    in_b, back_b = columns(in_b, 0, hidden), columns(back_b, 0, hidden)

    place = jnp.arange(width)
    relative = place // (2 * nz * block) + 2 * (place // (nz * block) % 2) + 4 * (place // block % nz)
    feature = (own ^ relative) * block + place % block
    order = cast_low(jnp.arange(width)[:, None] == feature[None, :])
    page = mine // copies

    def of_page(values):
        return lax.dynamic_index_in_dim(values, page, 0, keepdims=False)

    text = cast_low(matmul(of_page(text_rows), order))
    vision = cast_low(matmul(of_page(vision_rows), order))
    grad_in = matmul(from_owners(out_grad), order)
    keep_text, keep_patch = of_page(text_keep), of_page(patch_keep)
    segment_hot = (of_page(segment_ids)[:, None] == jnp.arange(segment_box.shape[1])).astype(f32)
    token_box = matmul(segment_hot, of_page(segment_box).astype(f32)).astype(jnp.int32)
    text_hot = cast_low(grid_hot(token_box))
    patch = jnp.arange(patches, dtype=jnp.int32)
    patch_hot = cast_low(grid_hot(jnp.stack([patch % GRID, patch // GRID], axis=1)))
    tables = jnp.stack([box_table_a, box_table_b])
    tables = [tables] + [swap(tables, 0, j) for j in range(1, nt)]
    tables = jnp.concatenate(tables, axis=1)
    heads = tables.shape[1]

    def own_parts(table):
        parts = cast_low(matmul(text_hot, pair_tables(table)))
        return jnp.transpose(parts.reshape(length, heads, 2 * GRID), (1, 0, 2))

    own_a, own_b = own_parts(tables[0]), own_parts(tables[1])

    qkv = cast_low(matmul(text, qkv_a))
    queries_a, keys_a, values_a = (qkv[:, i * width : (i + 1) * width] for i in range(3))
    context_a, lse_a = attend_forward(queries_a, keys_a, values_a, own_a, text_hot, keep_text)
    mixed_a, normed_a0, scale_a0 = norm_forward(
        text.astype(f32) + matmul_nt(context_a, out_a), gains[0], shifts[0]
    )
    mixed_low_a = cast_low(mixed_a)
    gelu_a, slope_a = gelu_pair(matmul(mixed_low_a, in_a))
    middle, normed_a1, scale_a1 = norm_forward(
        mixed_a + matmul_nt(gelu_a, back_a), gains[1], shifts[1]
    )
    middle_low = cast_low(middle)

    queries_b = cast_low(matmul(middle_low, query_b))
    kv = cast_low(matmul(vision, kv_b))
    keys_b, values_b = kv[:, :width], kv[:, width:]
    context_b, lse_b = attend_forward(queries_b, keys_b, values_b, own_b, patch_hot, keep_patch)
    mixed_b, normed_b0, scale_b0 = norm_forward(
        middle + matmul_nt(context_b, out_b), gains[2], shifts[2]
    )
    mixed_low_b = cast_low(mixed_b)
    gelu_b, slope_b = gelu_pair(matmul(mixed_low_b, in_b))
    final, normed_b1, scale_b1 = norm_forward(
        mixed_b + matmul_nt(gelu_b, back_b), gains[3], shifts[3]
    )
    layer_out = to_owners(cast_low(matmul_nt(cast_low(final), order)))

    pre_b, gain_b1, shift_b1 = norm_backward(grad_in, normed_b1, scale_b1, gains[3])
    branch_b = cast_low(pre_b)
    hidden_b = cast_low(matmul(branch_b, back_b) * slope_b.astype(f32))
    grad_mlp_b = scatter_rows([(branch_b, gelu_b)], [1])
    grad_in_b = scatter_rows([(mixed_low_b, hidden_b)], [1])
    mixed_grad_b = pre_b + matmul_nt(hidden_b, in_b)
    attn_pre_b, gain_b0, shift_b0 = norm_backward(mixed_grad_b, normed_b0, scale_b0, gains[2])
    attn_grad_b = cast_low(attn_pre_b)
    context_grad_b = cast_low(matmul(attn_grad_b, out_b))
    query_grad_b, key_grad_b, value_grad_b, right_b = attend_backward(
        queries_b, keys_b, values_b, own_b, patch_hot, keep_patch, lse_b, context_grad_b
    )
    kv_grad_b = jnp.concatenate([key_grad_b, value_grad_b], axis=1)
    grad_second = scatter_rows(
        [(middle_low, query_grad_b), (vision, kv_grad_b), (attn_grad_b, context_b)], [1, 2, 1]
    )
    middle_grad = attn_pre_b + matmul_nt(query_grad_b, query_b)
    vision_grad = matmul_nt(cast_low(matmul_nt(kv_grad_b, kv_b)), order)
    vision_grad = to_owners(cast_low(vision_grad)).astype(f32)

    pre_a, gain_a1, shift_a1 = norm_backward(middle_grad, normed_a1, scale_a1, gains[1])
    branch_a = cast_low(pre_a)
    hidden_a = cast_low(matmul(branch_a, back_a) * slope_a.astype(f32))
    grad_mlp_a = scatter_rows([(branch_a, gelu_a)], [1])
    grad_in_a = scatter_rows([(mixed_low_a, hidden_a)], [1])
    mixed_grad_a = pre_a + matmul_nt(hidden_a, in_a)
    attn_pre_a, gain_a0, shift_a0 = norm_backward(mixed_grad_a, normed_a0, scale_a0, gains[0])
    attn_grad_a = cast_low(attn_pre_a)
    context_grad_a = cast_low(matmul(attn_grad_a, out_a))
    query_grad_a, key_grad_a, value_grad_a, right_a = attend_backward(
        queries_a, keys_a, values_a, own_a, text_hot, keep_text, lse_a, context_grad_a
    )
    qkv_grad = jnp.concatenate([query_grad_a, key_grad_a, value_grad_a], axis=1)
    grad_first = scatter_rows([(text, qkv_grad), (attn_grad_a, context_a)], [3, 1])
    text_grad = cast_low(attn_pre_a + matmul_nt(qkv_grad, qkv_a))
    text_grad = to_owners(cast_low(matmul_nt(text_grad, order))).astype(f32)

    norm_grads = jnp.stack(
        [gain_a0, gain_a1, shift_a0, shift_a1, gain_b0, gain_b1, shift_b0, shift_b1]
    )
    norm_grads = jnp.transpose(norm_grads.reshape(8, 2, 2, nz, block), (1, 2, 3, 0, 4)) * (1.0 / copies)
    norm_sum = norm_grads[0] + swap(norm_grads[1], 1, 0)
    norm_sum = norm_sum[0] + swap(norm_sum[1], 2, 0)
    norm_sum = sum([swap(norm_sum[k], 4 * k, 0) for k in range(1, nz)], norm_sum[0])
    norm_sum = sum([swap(norm_sum, 0, j) for j in range(1, nt)], norm_sum)

    tables_grad = jnp.stack([table_grad(text_hot, right_a), table_grad(text_hot, right_b)])
    tables_grad = jnp.transpose(
        tables_grad.reshape(2, nt, heads // nt, 2, RELS) * (1.0 / copies), (1, 0, 2, 3, 4)
    )
    tables_grad = sum_all(tables_grad)

    return (
        layer_out,
        text_grad,
        vision_grad,
        grad_first[:, : 3 * share].reshape(block, 3, share),
        grad_first[:, 3 * share :].T,
        grad_in_a,
        grad_mlp_a.T,
        norm_sum[0:2],
        norm_sum[2:4],
        tables_grad[0],
        grad_second[:, :share],
        grad_second[:, share : 3 * share].reshape(block, 2, share),
        grad_second[:, 3 * share :].T,
        grad_in_b,
        grad_mlp_b.T,
        norm_sum[4:6],
        norm_sum[6:8],
        tables_grad[1],
    )


def solution(mesh):
    return jax.shard_map(
        shards,
        mesh=mesh,
        in_specs=(
            P("dp", None, None),
            P("dp", None, None),
            P("dp", None),
            P("dp", None),
            P("dp", None, None),
            P("dp", None),
            P("dp", None, "tensor"),
            P("tensor", "dp"),
            P("dp", "tensor"),
            P("tensor", "dp"),
            P(None, "dp"),
            P(None, "dp"),
            P("tensor", None, None),
            P("dp", "tensor"),
            P("dp", None, "tensor"),
            P("tensor", "dp"),
            P("dp", "tensor"),
            P("tensor", "dp"),
            P(None, "dp"),
            P(None, "dp"),
            P("tensor", None, None),
            P("dp", "tensor", None),
        ),
        out_specs=(
            P("dp", "tensor", None),
            P("dp", "tensor", None),
            P("dp", "tensor", None),
            P("dp", None, "tensor"),
            P("tensor", "dp"),
            P("dp", "tensor"),
            P("tensor", "dp"),
            P(None, "dp"),
            P(None, "dp"),
            P("tensor", None, None),
            P("dp", "tensor"),
            P("dp", None, "tensor"),
            P("tensor", "dp"),
            P("dp", "tensor"),
            P("tensor", "dp"),
            P(None, "dp"),
            P(None, "dp"),
            P("tensor", None, None),
        ),
        check_vma=False,
    )
```

```python
import functools

import jax
import jax.numpy as jnp
from jax import lax
from jax.experimental import pallas as pl
from jax.experimental.pallas import tpu as pltpu
from jax.sharding import PartitionSpec as P

HD = 64
GRID = 16
RELS = 2 * GRID - 1
LANES = 128
STRIP = 128

highest = lax.Precision.HIGHEST
epsilon = 1e-06
masked_score = -30000.0
mask_columns = (-29952.0, -48.0)
bf16 = jnp.bfloat16
f32 = jnp.float32
vmem = pltpu.CompilerParams(vmem_limit_bytes=16 * 2**20)


def cast_low(values):
    return values.astype(bf16)


def matmul(left_side, right_side):
    return jnp.dot(left_side, right_side, preferred_element_type=f32)


def matmul_tn(left_side, right_side):
    return lax.dot_general(
        left_side, right_side, (((0,), (0,)), ((), ())), preferred_element_type=f32
    )


def matmul_nt(left_side, right_side):
    return lax.dot_general(
        left_side, right_side, (((1,), (1,)), ((), ())), preferred_element_type=f32
    )


def gelu_pair(hidden):
    cdf = 0.5 + 0.5 * lax.erf(hidden * (0.5**0.5))
    slope = cdf + hidden * jnp.exp(-0.5 * hidden * hidden) * (0.3989422804014327)
    return cast_low(hidden * cdf), cast_low(slope)


def spread_tables(tables):
    n = tables.shape[0]
    lane = jnp.arange(LANES)
    dimension, offset = jnp.divmod(jnp.arange(2 * RELS), RELS)
    own = jnp.arange(GRID)[None, :, None]
    picks = (offset[:, None, None] == own - lane % GRID + GRID - 1) & (
        dimension[:, None, None] == lane // GRID
    )
    parts = matmul(tables, cast_low(picks).reshape(2 * RELS, GRID * LANES))
    parts = jnp.transpose(cast_low(parts).reshape(n, GRID, LANES), (1, 0, 2)).reshape(GRID, -1)
    lane = jnp.tile(lane, n)
    row = jnp.arange(LANES)[:, None]
    ones = cast_low((row == lane) & (row // 2 == GRID))
    parts = [jnp.where(lane // GRID == c, parts, jnp.zeros_like(parts)) for c in range(2)]
    return jnp.pad(jnp.concatenate(parts, axis=0), ((0, LANES - 2 * GRID), (0, 0))) + ones


def table_grad(pairs):
    pairs = pairs[:, : 2 * GRID, : 2 * GRID].reshape(-1, 2, GRID, 2, GRID)
    pairs = jnp.stack([pairs[:, 0, :, 0], pairs[:, 1, :, 1]], axis=1)
    offset = jnp.arange(GRID)[:, None] - jnp.arange(GRID)[None, :] + GRID - 1
    hot = (offset[:, :, None] == jnp.arange(RELS)).astype(f32)
    return jnp.einsum("hcab,abr->hcr", pairs, hot, precision=highest)


class Projection:
    def __init__(self, views, tile, start, tiles):
        self.views, self.tile, self.start, self.tiles = views, tile, start, tiles

    def arrays(self):
        return [array for share in self.views for array, _, _ in share]

    def specs(self):
        return [
            pl.BlockSpec((rows, self.tile), lambda t, at=at: (at, self.start + t))
            for share in self.views
            for _, at, rows in share
        ]

    def group(self, refs):
        refs, out = list(refs), []
        for share in self.views:
            out.append([refs.pop(0) for _ in share])
        return out, refs


def whole(array):
    return pl.BlockSpec(array.shape, lambda t: (0,) * array.ndim)


def tile_of(array):
    return pl.BlockSpec((None,) + array.shape[1:], lambda t: (t, 0, 0))


def joined(parts, axis):
    return parts[0] if len(parts) == 1 else jnp.concatenate(parts, axis=axis)


def strips(rows):
    return [pl.ds(start, STRIP) for start in range(0, rows, STRIP)]


def project(x, weight, how, slope=None):
    rows, width = x.shape
    count = len(weight.arrays())

    def kernel(x_ref, *refs):
        shares, refs = weight.group(refs)
        x = x_ref[...]
        out = joined([matmul(x, joined([r[...] for r in share], 0)) for share in shares], 1)
        if how == "gelu":
            refs[0][...], refs[1][...] = gelu_pair(out)
        elif how == "slope":
            refs[1][...] = cast_low(out * refs[0][...].astype(f32))
        else:
            refs[0][...] = cast_low(out)

    result = jax.ShapeDtypeStruct((weight.tiles, rows, width), bf16)
    extra = [] if slope is None else [slope]
    outs = [result] * (2 if how == "gelu" else 1)
    got = pl.pallas_call(
        kernel,
        grid=(weight.tiles,),
        in_specs=[whole(x)] + weight.specs() + [tile_of(e) for e in extra],
        out_specs=[tile_of(out) for out in outs],
        out_shape=outs,
        compiler_params=vmem,
        cost_estimate=pl.CostEstimate(
            flops=2 * rows * width * width * weight.tiles,
            bytes_accessed=2 * width * weight.tiles * (width + 2 * rows),
            transcendentals=0,
        ),
    )(x, *weight.arrays(), *extra)
    return got if how == "gelu" else got[0]


def project_back(h, weight, how, extra=(), params=None, at=()):
    tiles, rows, width = h.shape
    n_extra = len(extra) + (params is not None)

    def kernel(h_ref, *refs):
        shares, refs = weight.group(refs)
        extra, outs, sums = refs[:n_extra], refs[n_extra:-1], refs[-1]
        t = pl.program_id(0)
        h = h_ref[...]
        parts = []

        def param(i):
            return extra[-1][at[i] : at[i] + 1, :]

        def forward(cut):
            residual = extra[0][cut, :].astype(f32)
            if len(at) > 2:
                residual = residual * param(2) + param(3)
            values = sums[cut, :] + residual
            center = values - jnp.mean(values, axis=-1, keepdims=True)
            scale = lax.rsqrt(jnp.mean(center * center, axis=-1, keepdims=True) + epsilon)
            normed = center * scale
            return normed, scale, cast_low(normed * param(0) + param(1))

        def backward(grad, normed, scale):
            product = grad * normed
            grads = [jnp.sum(product, axis=0, keepdims=True), jnp.sum(grad, axis=0, keepdims=True)]
            scaled = grad * param(0)
            inner = scaled - jnp.mean(scaled, axis=-1, keepdims=True)
            inner = (inner - normed * jnp.mean(scaled * normed, axis=-1, keepdims=True)) * scale
            return inner, cast_low(inner), jnp.concatenate(grads, axis=0)

        for pieces in zip(*shares):
            parts.append(matmul_nt(h, joined([piece[...] for piece in pieces], 1)))
        total = joined(parts, 1)

        @pl.when(t == 0)
        def _():
            sums[...] = total

        @pl.when(t > 0)
        def _():
            sums[...] += total

        @pl.when(t == tiles - 1)
        def _():
            if how == "low":
                for cut in strips(rows):
                    outs[0][cut, :] = cast_low(sums[cut, :])
            elif how == "add":
                for cut in strips(rows):
                    outs[0][cut, :] = cast_low(sums[cut, :] + extra[0][cut, :])
            elif how == "norm":
                for cut in strips(rows):
                    normed, scale, result = forward(cut)
                    outs[0][cut, :] = normed
                    outs[1][cut, :] = scale
                    outs[2][cut, :] = result
                    outs[3][cut, :] = result[:, width // 2 :]
            else:
                param_grads = jnp.zeros((2, width), f32)
                for cut in strips(rows):
                    if how == "final":
                        normed, scale, result = forward(cut)
                        outs[0][cut, :] = result
                        grad = extra[1][cut, :].astype(f32)
                    else:
                        normed, scale = extra[1][cut, :], extra[2][cut, :]
                        grad = sums[cut, :] + extra[0][cut, :]
                    pre, low, strip_grads = backward(grad, normed, scale)
                    param_grads = param_grads + strip_grads
                    outs[-4][cut, :] = pre
                    outs[-3][cut, :] = low
                    outs[-2][cut, :] = low[:, width // 2 :]
                outs[-1][...] = param_grads

    low = jax.ShapeDtypeStruct((rows, width), bf16)
    wide = jax.ShapeDtypeStruct((rows, width), f32)
    part = jax.ShapeDtypeStruct((rows, width // 2), bf16)
    back = [wide, low, part, jax.ShapeDtypeStruct((2, width), f32)]
    outs = {
        "low": [low],
        "add": [low],
        "norm": [wide, jax.ShapeDtypeStruct((rows, 1), f32), low, part],
        "back": back,
        "final": [low] + back,
    }[how]
    extra = list(extra) + ([] if params is None else [params])
    got = pl.pallas_call(
        kernel,
        grid=(tiles,),
        in_specs=[tile_of(h)] + weight.specs() + [whole(e) for e in extra],
        out_specs=[whole(out) for out in outs],
        out_shape=outs,
        scratch_shapes=[pltpu.VMEM((rows, width), f32)],
        compiler_params=vmem,
        cost_estimate=pl.CostEstimate(
            flops=2 * rows * width * width * tiles,
            bytes_accessed=2 * width * tiles * (width + rows) + 12 * rows * width,
            transcendentals=0,
        ),
    )(h, *weight.arrays(), *extra)
    return got if len(outs) > 1 else got[0]


def weight_grad(products, factor, cut=None):
    width = products[0][0].shape[1]
    high = width // 2
    counts = [product[2].shape[0] for product in products]
    ends = [sum(counts[: i + 1]) for i in range(len(counts))]
    starts = [end - count for end, count in zip(ends, counts)]
    tiles = ends[-1]

    def kernel(*refs):
        sides = [refs[4 * i : 4 * i + 4] for i in range(len(products))]
        outs = refs[4 * len(products) : -len(products)]
        turned = refs[-len(products) :]
        t = pl.program_id(0)
        for (left, left_other, right, right_other), held, start, end in zip(sides, turned, starts, ends):

            @pl.when(t == start)
            def _():
                held[...] = jnp.concatenate([left[...].T, left_other[...].T], axis=1)

            @pl.when((t >= start) & (t < end))
            def _():
                total = matmul(held[...], jnp.concatenate([right[...], right_other[...]], axis=0))
                if factor != 1.0:
                    total = total * factor
                total = cast_low(total)
                if cut is None:
                    outs[0][...] = total
                    return
                rows, columns, strip = cut
                if strip:
                    outs[0][...] = total[rows : rows + strip, columns:]
                    outs[1][...] = total[rows + strip :, columns:]
                else:
                    outs[0][...] = total[rows:, columns:]
                outs[-3][...] = total[rows:, :columns]
                outs[-2][...] = total[:rows, columns:]
                outs[-1][...] = total[:rows, :columns]

    def column(rows, columns):
        return pl.BlockSpec((rows, columns), lambda t: (0, t))

    in_specs, args = [], []
    for product, start, count in zip(products, starts, counts):
        rows = product[0].shape[0]
        tile = pl.BlockSpec(
            (None, rows, width),
            lambda t, start=start, count=count: (jnp.clip(t - start, 0, count - 1), 0, 0),
        )
        in_specs += [pl.BlockSpec((rows, high), lambda t: (0, 0))] * 2 + [tile] * 2
        args += product
    if cut is None:
        parts = [(high, width)]
    else:
        rows, columns, strip = cut
        parts = [(strip, columns), (rows - strip, columns)] if strip else [(rows, columns)]
        parts = parts + [(rows, columns)] * 3
    outs = pl.pallas_call(
        kernel,
        grid=(tiles,),
        in_specs=in_specs,
        out_specs=[column(*part) for part in parts],
        out_shape=[jax.ShapeDtypeStruct((rows, tiles * columns), bf16) for rows, columns in parts],
        scratch_shapes=[pltpu.VMEM((high, 2 * product[0].shape[0]), bf16) for product in products],
        compiler_params=vmem,
        cost_estimate=pl.CostEstimate(
            flops=sum(4 * high * product[2].size for product in products),
            bytes_accessed=sum(4 * product[2].size + 2 * product[0].size for product in products)
            + 2 * tiles * high * width,
            transcendentals=0,
        ),
    )(*args)
    return outs[0] if cut is None else outs


def pair_of(array, role):
    return pl.BlockSpec((None, array.shape[1], LANES), lambda i: (role, 0, i))


def attend_forward(q, k, v, hot, spread, other, keep):
    (q, q_role), (k, k_role), (v, v_role) = q, k, v
    spread, first_pair = spread
    rows, n, width = q.shape[1], k.shape[1], q.shape[2]
    heads = width // HD

    def kernel(q_ref, k_ref, v_ref, hot_ref, spread_ref, other_ref, keep_ref, context_ref, probs_ref):
        keys = jnp.concatenate([k_ref[...] * keep_ref[...], other_ref[...]], axis=1)
        values = v_ref[...]
        first = lax.broadcasted_iota(jnp.int32, (rows, LANES), 1) < HD
        queries = q_ref[...] * jnp.asarray(HD**-0.5, bf16)
        parts = []
        for h in range(2):
            mine = jnp.where(first if h == 0 else ~first, queries, jnp.zeros_like(queries))
            bias = cast_low(matmul(hot_ref[...], spread_ref[:, h * LANES : (h + 1) * LANES]))
            scores = matmul_nt(jnp.concatenate([mine, bias], axis=1), keys)
            weights = jnp.exp(scores - jnp.max(scores, axis=1, keepdims=True))
            probs = cast_low(weights * (1.0 / jnp.sum(weights, axis=1, keepdims=True)))
            probs_ref[h] = probs
            parts.append(matmul(probs, values))
        context_ref[...] = cast_low(jnp.where(first, parts[0], parts[1]))

    probs = jax.ShapeDtypeStruct((heads, rows, n), bf16)
    return pl.pallas_call(
        kernel,
        grid=(heads // 2,),
        in_specs=[
            pair_of(q, q_role),
            pair_of(k, k_role),
            pair_of(v, v_role),
            whole(hot),
            pl.BlockSpec((LANES, 2 * LANES), lambda i: (0, first_pair + i)),
            whole(other),
            whole(keep),
        ],
        out_specs=[
            pl.BlockSpec((rows, LANES), lambda i: (0, i)),
            pl.BlockSpec((2, rows, n), lambda i: (i, 0, 0)),
        ],
        out_shape=[jax.ShapeDtypeStruct((rows, width), bf16), probs],
        compiler_params=vmem,
        cost_estimate=pl.CostEstimate(
            flops=8 * heads * rows * n * LANES,
            bytes_accessed=2 * heads * rows * n,
            transcendentals=heads * rows * n,
        ),
    )(q, k, v, hot, spread, other, keep)


def attend_backward(q, k, v, grad, probs, hot, other, keep):
    (q, q_role), (k, k_role), (v, v_role) = q, k, v
    rows, n, width = q.shape[1], k.shape[1], q.shape[2]
    heads = width // HD
    together = q is k

    def kernel(q_ref, k_ref, v_ref, grad_ref, probs_ref, hot_ref, other_ref, keep_ref, *refs):
        if together:
            grads_ref, pairs_ref, held_ref = refs
            dq_ref, dk_ref, dv_ref = (grads_ref.at[i] for i in range(3))
        else:
            dq_ref, dkv_ref, pairs_ref, held_ref = refs
            dk_ref, dv_ref = dkv_ref.at[0], dkv_ref.at[1]
        keep = keep_ref[...]
        keys = jnp.concatenate([k_ref[...] * keep, other_ref[...]], axis=1)
        values = v_ref[...]
        first = lax.broadcasted_iota(jnp.int32, (rows, LANES), 1) < HD
        grad = grad_ref[...]
        turned_queries = q_ref[...].T
        turned_grad = grad.T
        hot = hot_ref[...]
        query_parts, key_parts, value_parts = [], [], []
        for h in range(2):
            mine = jnp.where(first if h == 0 else ~first, grad, jnp.zeros_like(grad))
            prob_grad = matmul_nt(mine, values)
            probs = probs_ref[h].astype(f32)
            mean = jnp.sum(probs * prob_grad, axis=1, keepdims=True)
            held_ref[...] = cast_low(probs * (prob_grad - mean))
            both = matmul(held_ref[...], keys)
            query_parts.append(both[:, :LANES])
            right = both[:, LANES:]
            high = cast_low(right)
            rest = cast_low(right - high.astype(f32))
            pairs_ref[h] = matmul(hot, high) + matmul(hot, rest)
            mine = slice(h * HD, (h + 1) * HD)
            key_parts.append(matmul(turned_queries[mine], held_ref[...]))
            value_parts.append(matmul(turned_grad[mine], probs_ref[h]))
        dq_ref[...] = cast_low(jnp.where(first, query_parts[0], query_parts[1]) * HD**-0.5)
        turned = jnp.concatenate(key_parts, axis=0).T
        dk_ref[...] = cast_low(turned * HD**-0.5 * keep.astype(f32))
        dv_ref[...] = cast_low(jnp.concatenate(value_parts, axis=0).T)

    def grads_of(array):
        return pl.BlockSpec((array.shape[0], array.shape[1], LANES), lambda i: (0, 0, i))

    if together:
        outs = [jax.ShapeDtypeStruct((3, rows, width), bf16)]
    else:
        outs = [jax.ShapeDtypeStruct((1, rows, width), bf16), jax.ShapeDtypeStruct((2, n, width), bf16)]
    out_specs = [grads_of(out) for out in outs]
    if not together:
        out_specs[0] = pl.BlockSpec((None, rows, LANES), lambda i: (0, 0, i))
    outs.append(jax.ShapeDtypeStruct((heads, LANES, LANES), f32))
    out_specs.append(pl.BlockSpec((2, LANES, LANES), lambda i: (i, 0, 0)))
    return pl.pallas_call(
        kernel,
        grid=(heads // 2,),
        in_specs=[
            pair_of(q, q_role),
            pair_of(k, k_role),
            pair_of(v, v_role),
            pl.BlockSpec((rows, LANES), lambda i: (0, i)),
            pl.BlockSpec((2, rows, n), lambda i: (i, 0, 0)),
            whole(hot),
            whole(other),
            whole(keep),
        ],
        out_specs=out_specs,
        out_shape=outs,
        scratch_shapes=[pltpu.VMEM((rows, n), bf16)],
        compiler_params=vmem,
        cost_estimate=pl.CostEstimate(
            flops=20 * heads * rows * n * LANES, bytes_accessed=2 * heads * rows * n, transcendentals=0
        ),
    )(q, k, v, grad, probs, hot, other, keep)


ORDER = (
    "w1", "page", "w1", "page", "w2", "w1", "page", "w2", "w3", "w1", "page", "w3", "w4", "w1", "w2", "page", "w1", "layers", "w4", "w5", "w3", "layers", "w2", "w5", "w3", "+g6", "w4",
    "w2", "w5", "w6", "w3", "g6", "w2", "layers", "w3", "w6", "w4", "layers", "w4", "w5", "+g4", "w4", "w6", "layers", "g4", "w5", "w6", "+g3", "w5", "+g5", "w6", "layers", "w6",
    "layers", "+g1", "layers", "+g2", "g1", "layers", "layers", "+g1", "g2", "g3", "+g2", "layers", "layers", "+g4", "+g3", "g1", "g2", "g5", "g3", "g4", "g1", "layers",
    "g3", "g2", "out", "g1", "layers", "+g5", "g3", "g4", "g2", "g3", "+g6", "g5", "small", "vision", "g2", "small", "g4", "g5", "g6", "g4", "small", "small", "g1", "g6", "g3", "g5",
    "small", "g2", "small", "g6", "g5", "g6", "g4", "g1", "text", "g5", "g6",
)
WAYS = ("both", "both", "both", "both", "both", "both", "both", "both", "both", "both", "both", "both")


class Flows:
    def __init__(self, token):
        self.token = token
        self.flows, self.pending, self.results = {}, {}, {}

    def add(self, name, flow):
        self.flows[name] = flow
        self.pending[name] = next(flow)

    def step(self, *names):
        held = [self.pending[name] for name in names]
        held, self.token = lax.optimization_barrier((held, self.token))
        for name, arrays in zip(names, held):
            self.send(name, arrays)

    def send(self, name, arrays):
        try:
            self.pending[name] = self.flows[name].send(arrays)
        except StopIteration as end:
            self.results[name] = end.value


def shards(
    text_rows,
    vision_rows,
    segment_ids,
    text_keep,
    segment_box,
    patch_keep,
    attn_qkv_a,
    attn_out_a,
    mlp_in_a,
    mlp_out_a,
    norm_gain_a,
    norm_shift_a,
    box_table_a,
    attn_query_b,
    attn_kv_b,
    attn_out_b,
    mlp_in_b,
    mlp_out_b,
    norm_gain_b,
    norm_shift_b,
    box_table_b,
    out_grad,
):
    pages, length, width = text_rows.shape
    patches = vision_rows.shape[1]
    ndp, nt = lax.axis_size("dp"), lax.axis_size("tensor")
    own, mine = lax.axis_index("dp"), lax.axis_index("tensor")
    block = width // ndp
    share = attn_out_a.shape[0]
    tiles = mlp_in_a.shape[1] // share
    nz = ndp // 4
    z_bits = [range(3, ndp.bit_length() - 1), range(2, 3)]
    copies = nt // pages
    direct = nt == 2 and share % LANES == 0

    def swap(values, dp_mask, tensor_mask):
        pairs = [
            (d * nt + t, (d ^ dp_mask) * nt + (t ^ tensor_mask))
            for d in range(ndp)
            for t in range(nt)
        ]
        return lax.ppermute(values, ("dp", "tensor"), pairs)

    def in_order(relative):
        return [
            lax.select_n(mine, *[relative[a ^ m] for m in range(nt)])
            for a in range(nt)
        ]

    def gather_rows(piece, way="both"):
        (piece,) = yield [piece]
        for bits in z_bits:
            for bit in reversed(bits):
                others = [swap(piece, 1 << bit, 0)]
                if bit == bits[0]:
                    others = yield others
                piece = jnp.concatenate([piece, *others], axis=0)
        half = piece.shape[0] // 2
        if not direct or way == "xy":
            (along_x,) = yield [swap(piece, 2, 0)]
            near = jnp.concatenate([piece, along_x], axis=0)
            others = yield [swap(near, 0, j) for j in range(1, nt)]
            plane = jnp.concatenate([near, *others], axis=0)
        elif way == "yx":
            (along_y,) = yield [swap(piece, 0, 1)]
            near = jnp.concatenate([piece, along_y], axis=0)
            (far,) = yield [swap(near, 2, 0)]
            plane = jnp.concatenate([piece, far[: 2 * half], along_y, far[2 * half :]], axis=0)
        else:
            along_x, along_y = yield swap(piece, 2, 0), swap(piece, 0, 1)
            far = yield swap(along_y[:half], 2, 0), swap(along_x[half:], 0, 1)
            plane = jnp.concatenate([piece, along_x, along_y, *far], axis=0)
        plane, core = yield [plane, swap(plane, 1, 0)]
        return plane, core

    def projection(gathered, start, tiles):
        plane, core = gathered
        rows = width // 2
        if direct:
            views = [[(plane, j, rows), (core, j, rows)] for j in range(nt)]
            return Projection(views, share, start, tiles)
        plane, core = (
            array[:, start * share : (start + tiles) * share].reshape(nt, rows, tiles, share)
            for array in gathered
        )
        both = jnp.concatenate([plane, core], axis=1)
        both = jnp.transpose(both, (1, 2, 0, 3)).reshape(width, tiles * width)
        return Projection([[(both, 0, width)]], width, 0, tiles)

    def scatter_rows(count, way="both"):
        sides, others = {}, {}
        for _ in range(2):
            given = yield
            names = list(given)
            sides.update({name: given[name][0] for name in names})
            got = yield [swap(given[name][1], 1, 0) for name in names]
            others.update(zip(names, got))
        products = [
            (sides[p, "left"], others[p, "left"], sides[p, "right"], others[p, "right"])
            for p in range(count)
        ]
        high = width // 2
        rows = high // 2
        half = rows // 2
        if direct:
            cut = (rows, share, half if way == "both" else 0)
            parts = weight_grad(products, 1.0 / copies, cut)
            *far, near_x, near_y, here = parts
            if way == "both":
                from_x, from_y = yield swap(far[0], 2, 0), swap(far[1], 0, 1)
                near_y = jnp.concatenate([near_y[:half] + from_x, near_y[half:]], axis=0)
                near_x = jnp.concatenate([near_x[:half], near_x[half:] + from_y], axis=0)
                from_x, from_y = yield swap(near_x, 2, 0), swap(near_y, 0, 1)
                here = here.astype(f32) + from_x + from_y
            elif way == "xy":
                far, from_x = yield swap(far[0], 2, 0), swap(near_x, 2, 0)
                (from_y,) = yield [swap(near_y + far, 0, 1)]
                here = here.astype(f32) + from_x + from_y
            else:
                far, from_y = yield swap(far[0], 0, 1), swap(near_y, 0, 1)
                (from_x,) = yield [swap(near_x + far, 2, 0)]
                here = here.astype(f32) + from_x + from_y
        else:
            total = weight_grad(products, 1.0 / copies)
            total = total.reshape(2, rows, -1, nt, share)

            def part(x, j):
                return total[x, :, :, j].reshape(rows, -1)

            from_x = yield [swap(part(1, j), 2, 0) for j in range(nt)]
            here = [part(0, j) + from_x[j] for j in range(nt)]
            from_y = yield [swap(here[j], 0, j) for j in range(1, nt)]
            here = sum([got.astype(f32) for got in from_y], here[0].astype(f32))
        for bits in reversed(z_bits):
            for bit in bits:
                here = cast_low(here)
                half = here.shape[0] // 2
                got = [swap(here[half:], 1 << bit, 0)]
                if bit == bits[-1]:
                    got = yield got
                here = here[:half].astype(f32) + got[0]
        return here

    def to_owners(rows):
        cut = rows.shape[0] // nt
        parts = [rows[a * cut : (a + 1) * cut] for a in range(nt)]
        relative = in_order(parts)
        arrived = yield [relative[0]] + [swap(relative[k], 0, k) for k in range(1, nt)]
        return jnp.stack(in_order(arrived)[::copies])

    def page_parts():
        (rows_text, rows_vision, shares, ids, box, kept_text, kept_patch) = yield [
            text_rows, vision_rows, out_grad, segment_ids, segment_box, text_keep, patch_keep
        ]
        place = jnp.arange(width)
        relative = place // (2 * nz * block) + 2 * (place // (nz * block) % 2)
        for bit in range(2, ndp.bit_length() - 1):
            relative = relative + (1 << bit) * (place // (nz * block >> (bit - 1)) % 2)
        feature = (own ^ relative) * block + place % block
        order = cast_low(jnp.arange(width)[:, None] == feature[None, :])
        shares = in_order([shares[a // copies] for a in range(nt)])
        tables = jnp.stack([box_table_a, box_table_b])
        got = yield [
            order,
            [swap(tables, 0, j) for j in range(1, nt)],
            [swap(shares[j], 0, j) for j in range(1, nt)],
        ]
        order, other_tables, other_shares = got
        page = mine // copies

        def of_page(values):
            return lax.dynamic_index_in_dim(values, page, 0, keepdims=False)

        text = cast_low(matmul(of_page(rows_text), order))
        vision = cast_low(matmul(of_page(rows_vision), order))
        text, vision = yield text, vision

        lane = jnp.arange(LANES)
        target = jnp.where(lane < 2 * GRID, lane % GRID, 1)
        select = jnp.stack([lane // GRID == 0, lane // GRID == 1]).astype(f32)
        fill = (lane // 2 == GRID).astype(f32)
        segment_hot = (of_page(ids)[:, None] == jnp.arange(box.shape[1])).astype(f32)
        token_box = matmul(segment_hot, matmul(of_page(box).astype(f32), select) + fill)
        hot = cast_low(token_box == target)
        patch = jnp.arange(patches)[:, None]
        patch_box = jnp.where(lane // GRID == 0, patch % GRID, patch // GRID)
        patch_box = jnp.where(lane < 2 * GRID, patch_box, fill.astype(jnp.int32))
        patch_hot = cast_low(patch_box == target)

        def other_columns(hot, keep):
            kept = (keep > 0).astype(bf16)[:, None]
            score = jnp.where(lane == 2 * GRID, *[jnp.asarray(m, bf16) for m in mask_columns])
            other = hot * jnp.where(lane < 2 * GRID, kept, score * (1 - kept))
            return other, jnp.broadcast_to(kept, other.shape)

        other_a = other_columns(hot, of_page(kept_text))
        other_b = other_columns(patch_hot, of_page(kept_patch))
        tables = jnp.concatenate([tables] + other_tables, axis=1)
        spread = spread_tables(tables.reshape(-1, 2 * RELS))
        hot, turned, other_a, other_b, spread = yield hot, hot.T, other_a, other_b, spread
        grad_in = jnp.concatenate(in_order([shares[0]] + other_shares), axis=0)
        (grad_in,) = yield [cast_low(matmul(grad_in, order))]
        return order, text, vision, grad_in, hot, turned, other_a, other_b, spread

    flows = Flows(text_keep[0, 0])

    norms = jnp.concatenate([norm_gain_a, norm_shift_a, norm_gain_b, norm_shift_b], axis=0)
    norm_columns = jnp.pad(norms.T, ((0, 0), (0, LANES - norms.shape[0])))
    def weights(*pieces):
        return gather_rows(jnp.concatenate(pieces, axis=1))

    for name, way, pieces in (
        ("w1", WAYS[0], (attn_qkv_a.reshape(block, -1), norm_columns)),
        ("w2", WAYS[1], (attn_out_a.T, mlp_in_a)),
        ("w3", WAYS[2], (mlp_out_a.T,)),
        ("w4", WAYS[3], (attn_query_b, attn_kv_b.reshape(block, -1))),
        ("w5", WAYS[4], (attn_out_b.T, mlp_in_b)),
        ("w6", WAYS[5], (mlp_out_b.T,)),
    ):
        flows.add(name, gather_rows(jnp.concatenate(pieces, axis=1), way))
    flows.add("page", page_parts())
    for i, count in enumerate((1, 2, 2, 1, 2, 1)):
        flows.add(f"g{i + 1}", scatter_rows(count, WAYS[6 + i]))
    results = flows.results
    sides = {}
    tables_grads, norm_grads = {}, {}
    high = width // 2

    def chain():
        yield []
        order, text, vision, grad_in, hot, turned, other_a, other_b, spread = results["page"]
        pairs = spread.shape[1] // (4 * LANES)
        sides["g3"] = {(1, "left"): (vision, vision[:, high:])}
        sides["g6"] = {(0, "left"): (text, text[:, high:])}

        at = 3 * share
        gathered = results["w1"]
        norms = jnp.concatenate([part[:high, at : at + 8] for part in gathered], axis=0)
        (norms,) = yield [norms.T.astype(f32)]
        qkv_a = projection(gathered, 0, 3)
        qkv = project(text, qkv_a, "low")
        triple_a = ((qkv, 0), (qkv, 1), (qkv, 2))
        context_a, probs_a = yield attend_forward(*triple_a, hot, (spread, 0), *other_a)
        out_a, in_a = projection(results["w2"], 0, 1), projection(results["w2"], 1, tiles)
        normed_a0, scale_a0, mixed_a, part = project_back(
            context_a[None], out_a, "norm", [text], norms, (0, 2)
        )
        gelu_a, slope_a = yield project(mixed_a, in_a, "gelu")
        sides["g5"] = {
            (0, "right"): (context_a[None], context_a[None]),
            (1, "left"): (mixed_a, part),
        }
        sides["g4"] = {(0, "right"): (gelu_a, gelu_a)}
        back_a = projection(results["w3"], 0, tiles)
        normed_a1, scale_a1, middle, part = yield project_back(
            gelu_a, back_a, "norm", [normed_a0], norms, (1, 3, 0, 2)
        )
        sides["g3"][0, "left"] = (middle, part)

        query_b, kv_b = projection(results["w4"], 0, 1), projection(results["w4"], 1, 2)
        queries_b = project(middle, query_b, "low")
        kv = project(vision, kv_b, "low")
        triple_b = ((queries_b, 0), (kv, 0), (kv, 1))
        context_b, probs_b = yield attend_forward(*triple_b, hot, (spread, pairs), *other_b)
        out_b, in_b = projection(results["w5"], 0, 1), projection(results["w5"], 1, tiles)
        normed_b0, scale_b0, mixed_b, part = project_back(
            context_b[None], out_b, "norm", [normed_a1], norms, (4, 6, 1, 3)
        )
        gelu_b, slope_b = yield project(mixed_b, in_b, "gelu")
        sides["g2"] = {
            (0, "right"): (context_b[None], context_b[None]),
            (1, "left"): (mixed_b, part),
        }
        sides["g1"] = {(0, "right"): (gelu_b, gelu_b)}
        back_b = projection(results["w6"], 0, tiles)
        final, pre, branch, part, norm_grads["b1"] = yield project_back(
            gelu_b, back_b, "final", [normed_b0, grad_in], norms, (5, 7, 4, 6)
        )

        sides["g1"] = {(0, "left"): (branch, part)}
        flows.add("out", to_owners(cast_low(matmul_nt(final, order))))
        (hidden,) = yield [project(branch, back_b, "slope", slope_b)]
        pre, attn_grad, part, norm_grads["b0"] = project_back(
            hidden, in_b, "back", [pre, normed_b0, scale_b0], norms, (4,)
        )
        (context_grad,) = project(attn_grad, out_b, "low")
        pre, attn_grad, part, context_grad = yield pre, attn_grad, part, context_grad
        sides["g2"] = {(0, "left"): (attn_grad, part), (1, "right"): (hidden, hidden)}
        query_grad, kv_grad, sums = yield attend_backward(
            *triple_b, context_grad, probs_b, turned, *other_b
        )
        tables_grads["b"] = sums
        sides["g3"] = {
            (0, "right"): (query_grad, query_grad),
            (1, "right"): (kv_grad, kv_grad),
        }
        pre, branch, part, norm_grads["a1"] = project_back(
            query_grad, query_b, "back", [pre, normed_a1, scale_a1], norms, (1,)
        )
        hidden = project(branch, back_a, "slope", slope_a)
        pre, branch, part, hidden = yield pre, branch, part, hidden
        sides["g4"] = {(0, "left"): (branch, part)}
        vision_grad = project_back(kv_grad, kv_b, "low")
        flows.add("vision", to_owners(cast_low(matmul_nt(vision_grad, order))))
        pre, attn_grad, part, norm_grads["a0"] = project_back(
            hidden, in_a, "back", [pre, normed_a0, scale_a0], norms, (0,)
        )
        (context_grad,) = project(attn_grad, out_a, "low")
        pre, attn_grad, part, context_grad = yield pre, attn_grad, part, context_grad
        sides["g5"] = {(0, "left"): (attn_grad, part), (1, "right"): (hidden, hidden)}
        qkv_grad, sums = yield attend_backward(
            *triple_a, context_grad, probs_a, turned, *other_a
        )
        tables_grads["a"] = sums
        sides["g6"] = {(0, "right"): (qkv_grad, qkv_grad)}
        text_grad = project_back(qkv_grad, qkv_a, "add", [pre])
        flows.add("text", to_owners(cast_low(matmul_nt(text_grad, order))))
        flows.add("small", small_sums(tables_grads["a"], tables_grads["b"]))

    def small_sums(pairs_a, pairs_b):
        norms = jnp.concatenate([norm_grads[i] for i in ("a0", "a1", "b0", "b1")], axis=0)
        norms = jnp.transpose(norms.reshape(8, ndp, block), (1, 0, 2)).reshape(ndp, 8 * block)
        tables = jnp.stack([table_grad(pairs_a), table_grad(pairs_b)])
        heads = pairs_a.shape[0]
        tables = jnp.transpose(tables.reshape(2, nt, heads // nt, 2, RELS), (1, 0, 2, 3, 4))
        tables = tables.reshape(nt, -1)
        size = tables.shape[1]
        tables = jnp.pad(tables, ((0, 0), (0, -size % (8 * block)))).reshape(nt, -1, 8 * block)
        depth = tables.shape[1]
        tables = tables.reshape(nt * depth, 8 * block)
        norms, tables = yield norms * (1.0 / copies), tables * (1.0 / copies)
        for bits in (range(1), range(1, 2), *reversed(z_bits)):
            for bit in bits:
                half = norms.shape[0] // 2
                got = [swap(jnp.concatenate([norms[half:], tables], axis=0), 1 << bit, 0)]
                if bit == bits[-1]:
                    got = yield got
                norms, tables = norms[:half] + got[0][:half], tables + got[0][half:]
        others = yield [
            swap(jnp.concatenate([norms, tables[j * depth : (j + 1) * depth]], axis=0), 0, j)
            for j in range(1, nt)
        ]
        total = sum(others, jnp.concatenate([norms, tables[:depth]], axis=0))
        tables = total[1:].reshape(-1)[:size].reshape(2, heads // nt, 2, RELS)
        return total[0].reshape(8, block), tables

    flows.add("layers", chain())
    for name in ORDER:
        if name.startswith("+"):
            flows.send(name[1:], sides[name[1:]])
        else:
            flows.step(name)
    norm_sums, tables = results["small"]
    tables = tables + (flows.token - text_keep[0, 0]).astype(f32)
    grad_in_a, grad_in_b = results["g5"], results["g2"]
    grad_second = results["g3"]

    return (
        results["out"],
        results["text"].astype(f32),
        results["vision"].astype(f32),
        results["g6"].reshape(block, 3, share),
        grad_in_a[:, :share].T,
        grad_in_a[:, share:],
        results["g4"].T,
        norm_sums[0:4:2],
        norm_sums[1:4:2],
        tables[0],
        grad_second[:, :share],
        grad_second[:, share:].reshape(block, 2, share),
        grad_in_b[:, :share].T,
        grad_in_b[:, share:],
        results["g1"].T,
        norm_sums[4:8:2],
        norm_sums[5:8:2],
        tables[1],
    )


def solution(mesh):
    return jax.shard_map(
        shards,
        mesh=mesh,
        in_specs=(
            P("dp", None, None),
            P("dp", None, None),
            P("dp", None),
            P("dp", None),
            P("dp", None, None),
            P("dp", None),
            P("dp", None, "tensor"),
            P("tensor", "dp"),
            P("dp", "tensor"),
            P("tensor", "dp"),
            P(None, "dp"),
            P(None, "dp"),
            P("tensor", None, None),
            P("dp", "tensor"),
            P("dp", None, "tensor"),
            P("tensor", "dp"),
            P("dp", "tensor"),
            P("tensor", "dp"),
            P(None, "dp"),
            P(None, "dp"),
            P("tensor", None, None),
            P("dp", "tensor", None),
        ),
        out_specs=(
            P("dp", "tensor", None),
            P("dp", "tensor", None),
            P("dp", "tensor", None),
            P("dp", None, "tensor"),
            P("tensor", "dp"),
            P("dp", "tensor"),
            P("tensor", "dp"),
            P(None, "dp"),
            P(None, "dp"),
            P("tensor", None, None),
            P("dp", "tensor"),
            P("dp", None, "tensor"),
            P("tensor", "dp"),
            P("dp", "tensor"),
            P("tensor", "dp"),
            P(None, "dp"),
            P(None, "dp"),
            P("tensor", None, None),
        ),
        check_vma=False,
    )
```

```python
import functools

import jax
import jax.numpy as jnp
from jax import lax
from jax.experimental import pallas as pl
from jax.experimental.pallas import tpu as pltpu
from jax.sharding import PartitionSpec as P

HD = 64
GRID = 16
RELS = 2 * GRID - 1
LANES = 128
STRIP = 128

highest = lax.Precision.HIGHEST
epsilon = 1e-06
masked_score = -30000.0
mask_columns = (-29952.0, -48.0)
bf16 = jnp.bfloat16
f32 = jnp.float32
vmem = pltpu.CompilerParams(vmem_limit_bytes=16 * 2**20)


def cast_low(values):
    return values.astype(bf16)


def matmul(left_side, right_side):
    return jnp.dot(left_side, right_side, preferred_element_type=f32)


def matmul_tn(left_side, right_side):
    return lax.dot_general(
        left_side, right_side, (((0,), (0,)), ((), ())), preferred_element_type=f32
    )


def matmul_nt(left_side, right_side):
    return lax.dot_general(
        left_side, right_side, (((1,), (1,)), ((), ())), preferred_element_type=f32
    )


def gelu_pair(hidden):
    cdf = 0.5 + 0.5 * lax.erf(hidden * (0.5**0.5))
    slope = cdf + hidden * jnp.exp(-0.5 * hidden * hidden) * (0.3989422804014327)
    return cast_low(hidden * cdf), cast_low(slope)


def spread_tables(tables):
    n = tables.shape[0]
    lane = jnp.arange(LANES)
    dimension, offset = jnp.divmod(jnp.arange(2 * RELS), RELS)
    own = jnp.arange(GRID)[None, :, None]
    picks = (offset[:, None, None] == own - lane % GRID + GRID - 1) & (
        dimension[:, None, None] == lane // GRID
    )
    parts = matmul(tables, cast_low(picks).reshape(2 * RELS, GRID * LANES))
    parts = jnp.transpose(cast_low(parts).reshape(n, GRID, LANES), (1, 0, 2)).reshape(GRID, -1)
    lane = jnp.tile(lane, n)
    row = jnp.arange(LANES)[:, None]
    ones = cast_low((row == lane) & (row // 2 == GRID))
    parts = [jnp.where(lane // GRID == c, parts, jnp.zeros_like(parts)) for c in range(2)]
    return jnp.pad(jnp.concatenate(parts, axis=0), ((0, LANES - 2 * GRID), (0, 0))) + ones


def table_grad(pairs):
    pairs = pairs[:, : 2 * GRID, : 2 * GRID].reshape(-1, 2, GRID, 2, GRID)
    pairs = jnp.stack([pairs[:, 0, :, 0], pairs[:, 1, :, 1]], axis=1)
    offset = jnp.arange(GRID)[:, None] - jnp.arange(GRID)[None, :] + GRID - 1
    hot = (offset[:, :, None] == jnp.arange(RELS)).astype(f32)
    return jnp.einsum("hcab,abr->hcr", pairs, hot, precision=highest)


def in_hbm(array):
    return pltpu.with_memory_space_constraint(array, pltpu.HBM)


class Projection:
    def __init__(self, views, tile, start, tiles):
        self.views, self.tile, self.start, self.tiles = views, tile, start, tiles

    def arrays(self):
        return [in_hbm(array) for share in self.views for array, _, _ in share]

    def specs(self):
        return [
            pl.BlockSpec((rows, self.tile), lambda t, at=at: (at, self.start + t))
            for share in self.views
            for _, at, rows in share
        ]

    def read(self, refs):
        refs, shares = list(refs), []
        for share in self.views:
            shares.append(joined([refs.pop(0)[...] for _ in share], 0))
        return joined(shares, 1), refs


class BlocksProjection:
    def __init__(self, array, places, tile, start, tiles):
        self.array, self.places, self.tile, self.start, self.tiles = array, places, tile, start, tiles

    def arrays(self):
        return [self.places, in_hbm(self.array)]

    def specs(self):
        return [
            pl.BlockSpec(memory_space=pltpu.SMEM),
            pl.BlockSpec(
                self.array.shape[:2] + (self.tile,), lambda t: (0, 0, self.start + t)
            ),
        ]

    def read(self, refs):
        places, blocks, *refs = refs
        shares, count = self.places.shape
        parts = [[blocks[places[j, r]] for r in range(count)] for j in range(shares)]
        return joined([joined(part, 0) for part in parts], 1), refs


def whole(array):
    return pl.BlockSpec(array.shape, lambda t: (0,) * array.ndim)


def tile_of(array):
    return pl.BlockSpec((None,) + array.shape[1:], lambda t: (t, 0, 0))


def joined(parts, axis):
    return parts[0] if len(parts) == 1 else jnp.concatenate(parts, axis=axis)


def strips(rows):
    return [pl.ds(start, STRIP) for start in range(0, rows, STRIP)]


def project(x, weight, how, slope=None):
    rows, width = x.shape

    def kernel(x_ref, *refs):
        tile, refs = weight.read(refs)
        out = matmul(x_ref[...], tile)
        if how == "gelu":
            refs[0][...], refs[1][...] = gelu_pair(out)
        elif how == "slope":
            refs[1][...] = cast_low(out * refs[0][...].astype(f32))
        else:
            refs[0][...] = cast_low(out)

    result = jax.ShapeDtypeStruct((weight.tiles, rows, width), bf16)
    extra = [] if slope is None else [slope]
    outs = [result] * (2 if how == "gelu" else 1)
    got = pl.pallas_call(
        kernel,
        grid=(weight.tiles,),
        in_specs=[whole(x)] + weight.specs() + [tile_of(e) for e in extra],
        out_specs=[tile_of(out) for out in outs],
        out_shape=outs,
        compiler_params=vmem,
        cost_estimate=pl.CostEstimate(
            flops=2 * rows * width * width * weight.tiles,
            bytes_accessed=2 * width * weight.tiles * (width + 2 * rows),
            transcendentals=0,
        ),
    )(x, *weight.arrays(), *extra)
    return got if how == "gelu" else got[0]


def project_back(h, weight, how, extra=(), params=None, at=()):
    tiles, rows, width = h.shape
    n_extra = len(extra) + (params is not None)

    def kernel(h_ref, *refs):
        tile, refs = weight.read(refs)
        extra, outs, sums = refs[:n_extra], refs[n_extra:-1], refs[-1]
        t = pl.program_id(0)

        def param(i):
            return extra[-1][at[i] : at[i] + 1, :]

        def forward(cut):
            residual = extra[0][cut, :].astype(f32)
            if len(at) > 2:
                residual = residual * param(2) + param(3)
            values = sums[cut, :] + residual
            center = values - jnp.mean(values, axis=-1, keepdims=True)
            scale = lax.rsqrt(jnp.mean(center * center, axis=-1, keepdims=True) + epsilon)
            normed = center * scale
            return normed, scale, cast_low(normed * param(0) + param(1))

        def backward(grad, normed, scale):
            product = grad * normed
            grads = [jnp.sum(product, axis=0, keepdims=True), jnp.sum(grad, axis=0, keepdims=True)]
            scaled = grad * param(0)
            inner = scaled - jnp.mean(scaled, axis=-1, keepdims=True)
            inner = (inner - normed * jnp.mean(scaled * normed, axis=-1, keepdims=True)) * scale
            return inner, cast_low(inner), jnp.concatenate(grads, axis=0)

        total = matmul_nt(h_ref[...], tile)

        @pl.when(t == 0)
        def _():
            sums[...] = total

        @pl.when(t > 0)
        def _():
            sums[...] += total

        @pl.when(t == tiles - 1)
        def _():
            if how == "low":
                for cut in strips(rows):
                    outs[0][cut, :] = cast_low(sums[cut, :])
            elif how == "add":
                for cut in strips(rows):
                    outs[0][cut, :] = cast_low(sums[cut, :] + extra[0][cut, :])
            elif how == "norm":
                for cut in strips(rows):
                    normed, scale, result = forward(cut)
                    outs[0][cut, :] = normed
                    outs[1][cut, :] = scale
                    outs[2][cut, :] = result
                    outs[3][cut, :] = result[:, width // 2 :]
            else:
                param_grads = jnp.zeros((2, width), f32)
                for cut in strips(rows):
                    if how == "final":
                        normed, scale, result = forward(cut)
                        outs[0][cut, :] = result
                        grad = extra[1][cut, :].astype(f32)
                    else:
                        normed, scale = extra[1][cut, :], extra[2][cut, :]
                        grad = sums[cut, :] + extra[0][cut, :]
                    pre, low, strip_grads = backward(grad, normed, scale)
                    param_grads = param_grads + strip_grads
                    outs[-4][cut, :] = pre
                    outs[-3][cut, :] = low
                    outs[-2][cut, :] = low[:, width // 2 :]
                outs[-1][...] = param_grads

    low = jax.ShapeDtypeStruct((rows, width), bf16)
    wide = jax.ShapeDtypeStruct((rows, width), f32)
    part = jax.ShapeDtypeStruct((rows, width // 2), bf16)
    back = [wide, low, part, jax.ShapeDtypeStruct((2, width), f32)]
    outs = {
        "low": [low],
        "add": [low],
        "norm": [wide, jax.ShapeDtypeStruct((rows, 1), f32), low, part],
        "back": back,
        "final": [low] + back,
    }[how]
    extra = list(extra) + ([] if params is None else [params])
    got = pl.pallas_call(
        kernel,
        grid=(tiles,),
        in_specs=[tile_of(h)] + weight.specs() + [whole(e) for e in extra],
        out_specs=[whole(out) for out in outs],
        out_shape=outs,
        scratch_shapes=[pltpu.VMEM((rows, width), f32)],
        compiler_params=vmem,
        cost_estimate=pl.CostEstimate(
            flops=2 * rows * width * width * tiles,
            bytes_accessed=2 * width * tiles * (width + rows) + 12 * rows * width,
            transcendentals=0,
        ),
    )(h, *weight.arrays(), *extra)
    return got if len(outs) > 1 else got[0]


def weight_grad(products, factor, way=None):
    width = products[0][0].shape[1]
    high = width // 2
    rows, columns = high // 2, width // 2
    counts = [product[2].shape[0] for product in products]
    ends = [sum(counts[: i + 1]) for i in range(len(counts))]
    starts = [end - count for end, count in zip(ends, counts)]
    tiles = ends[-1]

    def kernel(*refs):
        sides = [refs[4 * i : 4 * i + 4] for i in range(len(products))]
        outs = refs[4 * len(products) : -len(products)]
        turned = refs[-len(products) :]
        t = pl.program_id(0)
        for (left, left_other, right, right_other), held, start, end in zip(sides, turned, starts, ends):

            @pl.when(t == start)
            def _():
                held[...] = jnp.concatenate([left[...].T, left_other[...].T], axis=1)

            @pl.when((t >= start) & (t < end))
            def _():
                total = matmul(held[...], jnp.concatenate([right[...], right_other[...]], axis=0))
                if factor != 1.0:
                    total = total * factor
                total = cast_low(total)
                if way is None:
                    outs[0][...] = total
                    return
                parts = {
                    (x, y): total[x * rows : (x + 1) * rows, y * columns : (y + 1) * columns]
                    for x in range(2)
                    for y in range(2)
                }
                if way == "both":
                    outs[0][...] = parts[1, 1][: rows // 2]
                    outs[1][...] = parts[1, 1][rows // 2 :]
                    outs[2][...] = parts[1, 0]
                    outs[3][...] = parts[0, 1]
                else:
                    other = (1, 0) if way == "xy" else (0, 1)
                    outs[0][:rows, :] = parts[1, 1]
                    outs[0][rows:, :] = parts[other]
                    outs[1][...] = parts[other[::-1]]
                outs[-1][...] = parts[0, 0]

    def column(rows, columns):
        return pl.BlockSpec((rows, columns), lambda t: (0, t))

    in_specs, args = [], []
    for product, start, count in zip(products, starts, counts):
        depth = product[0].shape[0]
        tile = pl.BlockSpec(
            (None, depth, width),
            lambda t, start=start, count=count: (jnp.clip(t - start, 0, count - 1), 0, 0),
        )
        in_specs += [pl.BlockSpec((depth, high), lambda t: (0, 0))] * 2 + [tile] * 2
        args += product
    if way is None:
        parts = [(high, width)]
    elif way == "both":
        parts = [(rows // 2, columns)] * 2 + [(rows, columns)] * 3
    else:
        parts = [(high, columns), (rows, columns), (rows, columns)]
    outs = pl.pallas_call(
        kernel,
        grid=(tiles,),
        in_specs=in_specs,
        out_specs=[column(*part) for part in parts],
        out_shape=[jax.ShapeDtypeStruct((rows, tiles * columns), bf16) for rows, columns in parts],
        scratch_shapes=[pltpu.VMEM((high, 2 * product[0].shape[0]), bf16) for product in products],
        compiler_params=vmem,
        cost_estimate=pl.CostEstimate(
            flops=sum(4 * high * product[2].size for product in products),
            bytes_accessed=sum(4 * product[2].size + 2 * product[0].size for product in products)
            + 2 * tiles * high * width,
            transcendentals=0,
        ),
    )(*args)
    return outs[0] if way is None else outs


def weight_grad_blocks(products, places):
    rows, width = products[0][0].shape
    shares, count = places.shape
    block, share = width // count, width // shares
    counts = [right.shape[0] for _, right in products]
    ends = [sum(counts[: i + 1]) for i in range(len(counts))]
    starts = [end - count for end, count in zip(ends, counts)]
    tiles = ends[-1]

    def kernel(places, *refs):
        out, turned = refs[2 * len(products)], refs[2 * len(products) + 1 :]
        t = pl.program_id(0)
        for i, (held, start, end) in enumerate(zip(turned, starts, ends)):

            @pl.when(t == start)
            def _():
                held[...] = refs[2 * i][...].T

            @pl.when((t >= start) & (t < end))
            def _():
                total = cast_low(matmul(held[...], refs[2 * i + 1][...]))
                for j in range(shares):
                    for r in range(count):
                        part = total[r * block : (r + 1) * block, j * share : (j + 1) * share]
                        out[places[j, r]] = part

    in_specs, args = [pl.BlockSpec(memory_space=pltpu.SMEM)], [places]
    for (left, right), start, depth in zip(products, starts, counts):
        tile = pl.BlockSpec(
            (None, rows, width),
            lambda t, start=start, depth=depth: (jnp.clip(t - start, 0, depth - 1), 0, 0),
        )
        in_specs += [whole(left), tile]
        args += [left, right]
    return pl.pallas_call(
        kernel,
        grid=(tiles,),
        in_specs=in_specs,
        out_specs=pl.BlockSpec((places.size, block, share), lambda t: (0, 0, t)),
        out_shape=jax.ShapeDtypeStruct((places.size, block, tiles * share), bf16),
        scratch_shapes=[pltpu.VMEM((width, rows), bf16) for _ in products],
        compiler_params=vmem,
        cost_estimate=pl.CostEstimate(
            flops=sum(2 * width * right.size for _, right in products),
            bytes_accessed=sum(2 * right.size for _, right in products) + 2 * tiles * width * width,
            transcendentals=0,
        ),
    )(*args)


def pair_of(array, role):
    return pl.BlockSpec((None, array.shape[1], LANES), lambda i: (role, 0, i))


def attend_forward(q, k, v, hot, spread, other, keep):
    (q, q_role), (k, k_role), (v, v_role) = q, k, v
    spread, first_pair = spread
    rows, n, width = q.shape[1], k.shape[1], q.shape[2]
    heads = width // HD

    def kernel(q_ref, k_ref, v_ref, hot_ref, spread_ref, other_ref, keep_ref, context_ref, probs_ref):
        keys = jnp.concatenate([k_ref[...] * keep_ref[...], other_ref[...]], axis=1)
        values = v_ref[...]
        first = lax.broadcasted_iota(jnp.int32, (rows, LANES), 1) < HD
        queries = q_ref[...] * jnp.asarray(HD**-0.5, bf16)
        parts = []
        for h in range(2):
            mine = jnp.where(first if h == 0 else ~first, queries, jnp.zeros_like(queries))
            bias = cast_low(matmul(hot_ref[...], spread_ref[:, h * LANES : (h + 1) * LANES]))
            scores = matmul_nt(jnp.concatenate([mine, bias], axis=1), keys)
            weights = jnp.exp(scores - jnp.max(scores, axis=1, keepdims=True))
            probs = cast_low(weights * (1.0 / jnp.sum(weights, axis=1, keepdims=True)))
            probs_ref[h] = probs
            parts.append(matmul(probs, values))
        context_ref[...] = cast_low(jnp.where(first, parts[0], parts[1]))

    probs = jax.ShapeDtypeStruct((heads, rows, n), bf16)
    return pl.pallas_call(
        kernel,
        grid=(heads // 2,),
        in_specs=[
            pair_of(q, q_role),
            pair_of(k, k_role),
            pair_of(v, v_role),
            whole(hot),
            pl.BlockSpec((LANES, 2 * LANES), lambda i: (0, first_pair + i)),
            whole(other),
            whole(keep),
        ],
        out_specs=[
            pl.BlockSpec((rows, LANES), lambda i: (0, i)),
            pl.BlockSpec((2, rows, n), lambda i: (i, 0, 0)),
        ],
        out_shape=[jax.ShapeDtypeStruct((rows, width), bf16), probs],
        compiler_params=vmem,
        cost_estimate=pl.CostEstimate(
            flops=8 * heads * rows * n * LANES,
            bytes_accessed=2 * heads * rows * n,
            transcendentals=heads * rows * n,
        ),
    )(q, k, v, hot, spread, other, keep)


def attend_backward(q, k, v, grad, probs, hot, other, keep):
    (q, q_role), (k, k_role), (v, v_role) = q, k, v
    rows, n, width = q.shape[1], k.shape[1], q.shape[2]
    heads = width // HD
    together = q is k

    def kernel(q_ref, k_ref, v_ref, grad_ref, probs_ref, hot_ref, other_ref, keep_ref, *refs):
        if together:
            grads_ref, pairs_ref, held_ref = refs
            dq_ref, dk_ref, dv_ref = (grads_ref.at[i] for i in range(3))
        else:
            dq_ref, dkv_ref, pairs_ref, held_ref = refs
            dk_ref, dv_ref = dkv_ref.at[0], dkv_ref.at[1]
        keep = keep_ref[...]
        keys = jnp.concatenate([k_ref[...] * keep, other_ref[...]], axis=1)
        values = v_ref[...]
        first = lax.broadcasted_iota(jnp.int32, (rows, LANES), 1) < HD
        grad = grad_ref[...]
        turned_queries = q_ref[...].T
        turned_grad = grad.T
        hot = hot_ref[...]
        query_parts, key_parts, value_parts = [], [], []
        for h in range(2):
            mine = jnp.where(first if h == 0 else ~first, grad, jnp.zeros_like(grad))
            prob_grad = matmul_nt(mine, values)
            probs = probs_ref[h].astype(f32)
            mean = jnp.sum(probs * prob_grad, axis=1, keepdims=True)
            held_ref[...] = cast_low(probs * (prob_grad - mean))
            both = matmul(held_ref[...], keys)
            query_parts.append(both[:, :LANES])
            right = both[:, LANES:]
            high = cast_low(right)
            rest = cast_low(right - high.astype(f32))
            pairs_ref[h] = matmul(hot, high) + matmul(hot, rest)
            mine = slice(h * HD, (h + 1) * HD)
            key_parts.append(matmul(turned_queries[mine], held_ref[...]))
            value_parts.append(matmul(turned_grad[mine], probs_ref[h]))
        dq_ref[...] = cast_low(jnp.where(first, query_parts[0], query_parts[1]) * HD**-0.5)
        turned = jnp.concatenate(key_parts, axis=0).T
        dk_ref[...] = cast_low(turned * HD**-0.5 * keep.astype(f32))
        dv_ref[...] = cast_low(jnp.concatenate(value_parts, axis=0).T)

    def grads_of(array):
        return pl.BlockSpec((array.shape[0], array.shape[1], LANES), lambda i: (0, 0, i))

    if together:
        outs = [jax.ShapeDtypeStruct((3, rows, width), bf16)]
    else:
        outs = [jax.ShapeDtypeStruct((1, rows, width), bf16), jax.ShapeDtypeStruct((2, n, width), bf16)]
    out_specs = [grads_of(out) for out in outs]
    if not together:
        out_specs[0] = pl.BlockSpec((None, rows, LANES), lambda i: (0, 0, i))
    outs.append(jax.ShapeDtypeStruct((heads, LANES, LANES), f32))
    out_specs.append(pl.BlockSpec((2, LANES, LANES), lambda i: (i, 0, 0)))
    return pl.pallas_call(
        kernel,
        grid=(heads // 2,),
        in_specs=[
            pair_of(q, q_role),
            pair_of(k, k_role),
            pair_of(v, v_role),
            pl.BlockSpec((rows, LANES), lambda i: (0, i)),
            pl.BlockSpec((2, rows, n), lambda i: (i, 0, 0)),
            whole(hot),
            whole(other),
            whole(keep),
        ],
        out_specs=out_specs,
        out_shape=outs,
        scratch_shapes=[pltpu.VMEM((rows, n), bf16)],
        compiler_params=vmem,
        cost_estimate=pl.CostEstimate(
            flops=20 * heads * rows * n * LANES, bytes_accessed=2 * heads * rows * n, transcendentals=0
        ),
    )(q, k, v, grad, probs, hot, other, keep)


GATHERS = (
    (("qkv",), "both"),
    (("outa", "ina",), "both"),
    (("mlpa",), "both"),
    (("q", "kv", "outb", "inb", "mlpb",), "blocks"),
)
SCATTERS = (
    (("mlpb", "inb",), "blocks"),
    (("q", "kv", "outb", "mlpa",), "both"),
    (("ina", "outa",), "both"),
    (("qkv",), "both"),
)

PAGE, LAYERS, OUT, VISION, TEXT, SMALL, W1, W2, W3, W4, G1, G2, G3, G4 = range(1, 15)
GATHER, SCATTER = W1, G1

ORDER = (
    W1, PAGE, W1, W1, PAGE, W2, W2, W1, PAGE, W3, W1, W2, PAGE, W1, PAGE, W3, LAYERS, LAYERS,
    LAYERS, W2, W3, W2, W2, LAYERS, LAYERS, W3, W3, W3, LAYERS, W4, LAYERS, LAYERS, LAYERS,
    LAYERS, LAYERS, LAYERS, LAYERS, -G1, OUT, -G2, LAYERS, G2, LAYERS, LAYERS, VISION, -G2, G2,
    LAYERS, -G3, G3, -G4, G4, G2, LAYERS, -G3, G3, G2, LAYERS, -G4, G3, G2, TEXT, G4, G3, SMALL,
    SMALL, G2, G4, SMALL, G3, SMALL, G4, SMALL, G3, G4, SMALL, G4, G1,
)


class Flows:
    def __init__(self, token):
        self.token = token
        self.flows, self.pending, self.results = {}, {}, {}

    def add(self, name, flow):
        self.flows[name] = flow
        self.pending[name] = next(flow)

    def step(self, *names):
        held = [self.pending[name] for name in names]
        held, self.token = lax.optimization_barrier((held, self.token))
        for name, arrays in zip(names, held):
            self.send(name, arrays)

    def mark(self, values):
        values, self.token = lax.optimization_barrier((values, self.token))
        return values

    def send(self, name, arrays):
        try:
            arrays = self.flows[name].send(arrays)
            self.pending[name] = self.mark(arrays) if name == LAYERS else arrays
        except StopIteration as end:
            self.results[name] = end.value


def shards(
    text_rows,
    vision_rows,
    segment_ids,
    text_keep,
    segment_box,
    patch_keep,
    attn_qkv_a,
    attn_out_a,
    mlp_in_a,
    mlp_out_a,
    norm_gain_a,
    norm_shift_a,
    box_table_a,
    attn_query_b,
    attn_kv_b,
    attn_out_b,
    mlp_in_b,
    mlp_out_b,
    norm_gain_b,
    norm_shift_b,
    box_table_b,
    out_grad,
):
    pages, length, width = text_rows.shape
    patches = vision_rows.shape[1]
    ndp, nt = lax.axis_size("dp"), lax.axis_size("tensor")
    own, mine = lax.axis_index("dp"), lax.axis_index("tensor")
    block = width // ndp
    share = attn_out_a.shape[0]
    tiles = mlp_in_a.shape[1] // share
    nz = ndp // 4
    z_bits = [range(3, ndp.bit_length() - 1), range(2, 3)]
    copies = nt // pages
    direct = nt == 2 and share % LANES == 0

    def swap(values, dp_mask, tensor_mask):
        pairs = [
            (d * nt + t, (d ^ dp_mask) * nt + (t ^ tensor_mask))
            for d in range(ndp)
            for t in range(nt)
        ]
        return lax.ppermute(flows.mark(values), ("dp", "tensor"), pairs)

    def in_order(relative):
        return [
            lax.select_n(mine, *[relative[a ^ m] for m in range(nt)])
            for a in range(nt)
        ]

    def gather_rows(piece, way):
        (piece,) = yield [piece]
        for bits in z_bits:
            for bit in reversed(bits):
                others = [swap(piece, 1 << bit, 0)]
                if bit == bits[0]:
                    others = yield others
                piece = jnp.concatenate([piece, *others], axis=0)
        rows = piece.shape[0]
        half = rows // 2

        if direct and way == "both":
            along_x, along_y = yield swap(piece, 2, 0), swap(piece, 0, 1)
            first = (piece, along_x, along_y)
            *far, piece_c, along_x_c, along_y_c = yield (
                swap(along_y[:half], 2, 0),
                swap(along_x[half:], 0, 1),
                *[swap(array, 1, 0) for array in first],
            )
            far_c = yield [swap(array, 1, 0) for array in far]
            return [
                [(array, 0, rows) for array in (piece, along_x, piece_c, along_x_c)],
                [(along_y, 0, rows)]
                + [(array, 0, half) for array in far]
                + [(along_y_c, 0, rows)]
                + [(array, 0, half) for array in far_c],
            ]
        if direct and way == "yx":
            (along_y,) = yield [swap(piece, 0, 1)]
            near = jnp.concatenate([piece, along_y], axis=0)
            far, near_c = yield swap(near, 2, 0), swap(near, 1, 0)
            (far_c,) = yield [swap(far, 1, 0)]
            return [[(array, j, rows) for array in (near, far, near_c, far_c)] for j in range(2)]
        (along_x,) = yield [swap(piece, 2, 0)]
        near = jnp.concatenate([piece, along_x], axis=0)
        near_c, *others = yield [swap(near, 1, 0)] + [swap(near, 0, j) for j in range(1, nt)]
        others_c = yield [swap(array, 1, 0) for array in others]
        return [
            [(array, 0, 2 * rows), (array_c, 0, 2 * rows)]
            for array, array_c in zip([near, *others], [near_c, *others_c])
        ]

    def projection(*names):
        group = next(group for group in gathers if names[0] in group)
        views = results[gathers[group]]
        counts = [pieces[name].shape[1] // share for name in group]
        first = group.index(names[0])
        start, tiles = sum(counts[:first]), sum(counts[first : first + len(names)])
        if not isinstance(views, list):
            return BlocksProjection(views, places, share, start, tiles)
        if direct:
            return Projection(views, share, start, tiles)
        shares = [
            jnp.concatenate([array[:, start * share : (start + tiles) * share] for array, _, _ in part], axis=0)
            for part in views
        ]
        both = jnp.stack([part.reshape(width, tiles, share) for part in shares], axis=2)
        return Projection([[(both.reshape(width, tiles * width), 0, width)]], width, 0, tiles)

    def at_once(flow, arrays):
        try:
            while True:
                arrays = flow.send(arrays)
        except StopIteration as end:
            return end.value

    def gather_blocks(piece):
        if direct:
            (blocks,) = yield [lax.all_gather(flows.mark(piece), ("dp", "tensor"))]
            return blocks
        (piece,) = yield [piece]
        flow = gather_rows(piece, "xy")
        return at_once(flow, next(flow))

    def scatter_blocks(names):
        sides = yield
        if direct:
            held = {key: array for key, (array, _) in sides.items()}
            products = [(held[name, "left"], held[name, "right"]) for name in names]
            parts = weight_grad_blocks(products, places)
            parts = flows.mark(parts.reshape(-1, parts.shape[2]))
            (out,) = yield [
                lax.psum_scatter(parts, ("dp", "tensor"), scatter_dimension=0, tiled=True)
            ]
            return out.astype(f32)
        yield []
        flow = scatter_rows(names, "xy")
        next(flow)
        flow.send(flow.send(sides))
        return at_once(flow, {})

    def scatter_rows(names, way):
        held, others = {}, {}
        for _ in range(2):
            given = yield
            held.update({key: array for key, (array, _) in given.items()})
            got = yield [swap(part, 1, 0) for _, part in given.values()]
            others.update(zip(given, got))
        products = [
            tuple(found[name, side] for side in ("left", "right") for found in (held, others))
            for name in names
        ]
        rows = width // 4
        half = rows // 2
        if direct:
            away, *near, here = weight_grad(products, 1.0 / copies, way)
            if way == "both":
                far_y, near_x, near_y = near
                from_x, from_y = yield swap(away, 2, 0), swap(far_y, 0, 1)
                near_y = lax.dynamic_update_slice(near_y, near_y[:half] + from_x, (0, 0))
                near_x = lax.dynamic_update_slice(near_x, near_x[half:] + from_y, (half, 0))
                got = yield swap(near_x, 2, 0), swap(near_y, 0, 1)
            else:
                masks = ((2, 0), (0, 1)) if way == "xy" else ((0, 1), (2, 0))
                (came,) = yield [swap(away, *masks[0])]
                (other,) = yield [swap(near[0] + came[:rows], *masks[1])]
                got = [came[rows:], other]
        else:
            total = weight_grad(products, 1.0 / copies).reshape(2, rows, -1, nt, share)
            parts = [[total[x, :, :, j].reshape(rows, -1) for j in range(nt)] for x in range(2)]
            from_x = yield [swap(part, 2, 0) for part in parts[1]]
            near = [part + came for part, came in zip(parts[0], from_x)]
            here = near[0]
            got = yield [swap(near[j], 0, j) for j in range(1, nt)]
        for bits in reversed(z_bits):
            for bit in bits:
                half = here.shape[0] // 2
                away = sum([part[half:] for part in got], here[half:].astype(f32))
                here = sum([part[:half] for part in got], here[:half].astype(f32))
                got = [swap(cast_low(away), 1 << bit, 0)]
                if bit == bits[-1]:
                    got = yield got
        return here + got[0]

    def to_owners(rows):
        cut = rows.shape[0] // nt
        parts = [rows[a * cut : (a + 1) * cut] for a in range(nt)]
        relative = in_order(parts)
        arrived = yield [relative[0]] + [swap(relative[k], 0, k) for k in range(1, nt)]
        return jnp.stack(in_order(arrived)[::copies])

    def page_parts():
        (rows_text, rows_vision, shares, ids, box, kept_text, kept_patch) = yield [
            text_rows, vision_rows, out_grad, segment_ids, segment_box, text_keep, patch_keep
        ]
        feature = source * block + jnp.arange(width) % block
        order = cast_low(jnp.arange(width)[:, None] == feature[None, :])
        shares = in_order([shares[a // copies] for a in range(nt)])
        tables = jnp.stack([box_table_a, box_table_b])
        got = yield [
            order,
            [swap(tables, 0, j) for j in range(1, nt)],
            [swap(shares[j], 0, j) for j in range(1, nt)],
        ]
        order, other_tables, other_shares = got
        page = mine // copies

        def of_page(values):
            return lax.dynamic_index_in_dim(values, page, 0, keepdims=False)

        text = cast_low(matmul(of_page(rows_text), order))
        vision = cast_low(matmul(of_page(rows_vision), order))
        text, vision = yield text, vision

        lane = jnp.arange(LANES)
        target = jnp.where(lane < 2 * GRID, lane % GRID, 1)
        select = jnp.stack([lane // GRID == 0, lane // GRID == 1]).astype(f32)
        fill = (lane // 2 == GRID).astype(f32)
        segment_hot = (of_page(ids)[:, None] == jnp.arange(box.shape[1])).astype(f32)
        token_box = matmul(segment_hot, matmul(of_page(box).astype(f32), select) + fill)
        hot = cast_low(token_box == target)
        patch = jnp.arange(patches)[:, None]
        patch_box = jnp.where(lane // GRID == 0, patch % GRID, patch // GRID)
        patch_box = jnp.where(lane < 2 * GRID, patch_box, fill.astype(jnp.int32))
        patch_hot = cast_low(patch_box == target)

        def other_columns(hot, keep):
            kept = (keep > 0).astype(bf16)[:, None]
            score = jnp.where(lane == 2 * GRID, *[jnp.asarray(m, bf16) for m in mask_columns])
            other = hot * jnp.where(lane < 2 * GRID, kept, score * (1 - kept))
            return other, jnp.broadcast_to(kept, other.shape)

        other_a = other_columns(hot, of_page(kept_text))
        other_b = other_columns(patch_hot, of_page(kept_patch))
        tables = jnp.concatenate([tables] + other_tables, axis=1)
        spread = spread_tables(tables.reshape(-1, 2 * RELS))
        hot, turned, other_a, other_b, spread = yield hot, hot.T, other_a, other_b, spread
        grad_in = jnp.concatenate(in_order([shares[0]] + other_shares), axis=0)
        (grad_in,) = yield [cast_low(matmul(grad_in, order))]
        return order, text, vision, grad_in, hot, turned, other_a, other_b, spread

    at = jnp.arange(width) // block
    relative = at // (2 * nz) + 2 * (at // nz % 2)
    for bit in range(2, ndp.bit_length() - 1):
        relative = relative + (1 << bit) * (at // (nz >> (bit - 1)) % 2)
    source = own ^ relative
    places = source[::block] * nt + (mine ^ jnp.arange(nt, dtype=jnp.int32))[:, None]

    flows = Flows(text_keep[0, 0])

    norms = jnp.concatenate([norm_gain_a, norm_shift_a, norm_gain_b, norm_shift_b], axis=0)
    norm_columns = jnp.pad(norms.T, ((0, 0), (0, LANES - norms.shape[0])))
    def weights(*pieces):
        return gather_rows(jnp.concatenate(pieces, axis=1))

    pieces = {
        "qkv": attn_qkv_a.reshape(block, -1),
        "outa": attn_out_a.T,
        "ina": mlp_in_a,
        "mlpa": mlp_out_a.T,
        "q": attn_query_b,
        "kv": attn_kv_b.reshape(block, -1),
        "outb": attn_out_b.T,
        "inb": mlp_in_b,
        "mlpb": mlp_out_b.T,
    }
    gathers, scatters = {}, {}
    for i, (group, way) in enumerate(GATHERS):
        gathers[group] = GATHER + i
        own_pieces = [pieces[name] for name in group] + [norm_columns] * ("qkv" in group)
        piece = jnp.concatenate(own_pieces, axis=1)
        gather = gather_blocks(piece) if way == "blocks" else gather_rows(piece, way)
        flows.add(gathers[group], gather)
    flows.add(PAGE, page_parts())
    for i, (group, way) in enumerate(SCATTERS):
        scatters[group] = SCATTER + i
        scatter = scatter_blocks(group) if way == "blocks" else scatter_rows(group, way)
        flows.add(scatters[group], scatter)
    results = flows.results
    sides, sent = {}, set()
    tables_grads, norm_grads = {}, {}
    high = width // 2

    def given(flow):
        group = next(group for group, name in scatters.items() if name == flow)
        ready = {key: side for key, side in sides.items() if key[0] in group and key not in sent}
        sent.update(ready)
        return ready

    def chain():
        yield []
        order, text, vision, grad_in, hot, turned, other_a, other_b, spread = results[PAGE]
        pairs = spread.shape[1] // (4 * LANES)
        sides["kv", "left"] = (vision, vision[:, high:])
        sides["qkv", "left"] = (text, text[:, high:])

        group = next(group for group in gathers if "qkv" in group)
        at = sum(pieces[name].shape[1] for name in group)
        norms = [
            array[i * rows : (i + 1) * rows, at : at + 8]
            for array, i, rows in results[gathers[group]][0]
        ]
        (norms,) = yield [jnp.concatenate(norms, axis=0).T.astype(f32)]
        qkv_a = projection("qkv")
        (qkv,) = yield [project(text, qkv_a, "low")]
        triple_a = ((qkv, 0), (qkv, 1), (qkv, 2))
        context_a, probs_a = yield attend_forward(*triple_a, hot, (spread, 0), *other_a)
        out_a = projection("outa")
        normed_a0, scale_a0, mixed_a, part = yield project_back(
            context_a[None], out_a, "norm", [text], norms, (0, 2)
        )
        sides["outa", "right"] = (context_a[None], context_a[None])
        sides["ina", "left"] = (mixed_a, part)
        in_a = projection("ina")
        gelu_a, slope_a = yield project(mixed_a, in_a, "gelu")
        sides["mlpa", "right"] = (gelu_a, gelu_a)
        back_a = projection("mlpa")
        normed_a1, scale_a1, middle, part = yield project_back(
            gelu_a, back_a, "norm", [normed_a0], norms, (1, 3, 0, 2)
        )
        sides["q", "left"] = (middle, part)

        query_b, kv_b = projection("q"), projection("kv")
        queries_b, kv = yield project(middle, query_b, "low"), project(vision, kv_b, "low")
        triple_b = ((queries_b, 0), (kv, 0), (kv, 1))
        context_b, probs_b = yield attend_forward(*triple_b, hot, (spread, pairs), *other_b)
        out_b = projection("outb")
        normed_b0, scale_b0, mixed_b, part = yield project_back(
            context_b[None], out_b, "norm", [normed_a1], norms, (4, 6, 1, 3)
        )
        sides["outb", "right"] = (context_b[None], context_b[None])
        sides["inb", "left"] = (mixed_b, part)
        in_b = projection("inb")
        gelu_b, slope_b = yield project(mixed_b, in_b, "gelu")
        sides["mlpb", "right"] = (gelu_b, gelu_b)
        back_b = projection("mlpb")
        final, pre, branch, part, norm_grads["b1"] = yield project_back(
            gelu_b, back_b, "final", [normed_b0, grad_in], norms, (5, 7, 4, 6)
        )

        sides["mlpb", "left"] = (branch, part)
        flows.add(OUT, to_owners(cast_low(matmul_nt(final, order))))
        (hidden,) = yield [project(branch, back_b, "slope", slope_b)]
        sides["inb", "right"] = (hidden, hidden)
        pre, attn_grad, part, norm_grads["b0"] = project_back(
            hidden, in_b, "back", [pre, normed_b0, scale_b0], norms, (4,)
        )
        (context_grad,) = project(attn_grad, out_b, "low")
        pre, attn_grad, part, context_grad = yield pre, attn_grad, part, context_grad
        sides["outb", "left"] = (attn_grad, part)
        query_grad, kv_grad, tables_grads["b"] = yield attend_backward(
            *triple_b, context_grad, probs_b, turned, *other_b
        )
        sides["q", "right"] = (query_grad, query_grad)
        sides["kv", "right"] = (kv_grad, kv_grad)
        vision_grad = project_back(kv_grad, kv_b, "low")
        flows.add(VISION, to_owners(cast_low(matmul_nt(vision_grad, order))))
        pre, branch, part, norm_grads["a1"] = yield project_back(
            query_grad, query_b, "back", [pre, normed_a1, scale_a1], norms, (1,)
        )
        sides["mlpa", "left"] = (branch, part)
        (hidden,) = yield [project(branch, back_a, "slope", slope_a)]
        sides["ina", "right"] = (hidden, hidden)
        pre, attn_grad, part, norm_grads["a0"] = project_back(
            hidden, in_a, "back", [pre, normed_a0, scale_a0], norms, (0,)
        )
        (context_grad,) = project(attn_grad, out_a, "low")
        pre, attn_grad, part, context_grad = yield pre, attn_grad, part, context_grad
        sides["outa", "left"] = (attn_grad, part)
        qkv_grad, tables_grads["a"] = yield attend_backward(
            *triple_a, context_grad, probs_a, turned, *other_a
        )
        sides["qkv", "right"] = (qkv_grad, qkv_grad)
        text_grad = project_back(qkv_grad, qkv_a, "add", [pre])
        flows.add(TEXT, to_owners(cast_low(matmul_nt(text_grad, order))))
        flows.add(SMALL, small_sums(order))

    def small_sums(order):
        norms = jnp.concatenate([norm_grads[i] for i in ("a0", "a1", "b0", "b1")], axis=0)
        norms = lax.dot_general(
            norms, order.astype(f32), (((1,), (1,)), ((), ())), precision=highest, preferred_element_type=f32
        )
        tables = jnp.stack([table_grad(tables_grads["a"]), table_grad(tables_grads["b"])])
        kept = (2, tables.shape[1] // nt, 2, RELS)
        tables = tables.reshape(2, nt, -1)
        size = 2 * tables.shape[2]
        tables = jnp.stack(in_order([tables[:, j].reshape(size) for j in range(nt)]))
        total = jnp.concatenate([norms, jnp.pad(tables, ((0, 0), (0, width - size)))], axis=0)
        (total,) = yield [total * (1.0 / copies)]
        for bits in (range(1), range(1, 2), *z_bits):
            for bit in bits:
                got = [swap(total, 1 << bit, 0)]
                if bit == bits[-1]:
                    got = yield got
                total = total + got[0]
        got = yield [swap(total, 0, j) for j in range(1, nt)]
        total = sum(got, total)
        norms = lax.dynamic_slice(total, (0, own * block), (8, block))
        tables = lax.dynamic_slice(total, (8 + mine, 0), (1, size))
        return norms, tables.reshape(kept)

    flows.add(LAYERS, chain())
    for name in ORDER:
        if name < 0:
            flows.send(-name, given(-name))
        else:
            flows.step(name)
    norm_sums, tables = results[SMALL]
    tables = tables + (flows.token - text_keep[0, 0]).astype(f32)
    grads = {}
    for group, flow in scatters.items():
        start = 0
        for name in group:
            size = pieces[name].shape[1]
            grads[name] = results[flow][:, start : start + size]
            start += size

    return (
        results[OUT],
        results[TEXT].astype(f32),
        results[VISION].astype(f32),
        grads["qkv"].reshape(block, 3, share),
        grads["outa"].T,
        grads["ina"],
        grads["mlpa"].T,
        norm_sums[0:4:2],
        norm_sums[1:4:2],
        tables[0],
        grads["q"],
        grads["kv"].reshape(block, 2, share),
        grads["outb"].T,
        grads["inb"],
        grads["mlpb"].T,
        norm_sums[4:8:2],
        norm_sums[5:8:2],
        tables[1],
    )


def solution(mesh):
    return jax.shard_map(
        shards,
        mesh=mesh,
        in_specs=(
            P("dp", None, None),
            P("dp", None, None),
            P("dp", None),
            P("dp", None),
            P("dp", None, None),
            P("dp", None),
            P("dp", None, "tensor"),
            P("tensor", "dp"),
            P("dp", "tensor"),
            P("tensor", "dp"),
            P(None, "dp"),
            P(None, "dp"),
            P("tensor", None, None),
            P("dp", "tensor"),
            P("dp", None, "tensor"),
            P("tensor", "dp"),
            P("dp", "tensor"),
            P("tensor", "dp"),
            P(None, "dp"),
            P(None, "dp"),
            P("tensor", None, None),
            P("dp", "tensor", None),
        ),
        out_specs=(
            P("dp", "tensor", None),
            P("dp", "tensor", None),
            P("dp", "tensor", None),
            P("dp", None, "tensor"),
            P("tensor", "dp"),
            P("dp", "tensor"),
            P("tensor", "dp"),
            P(None, "dp"),
            P(None, "dp"),
            P("tensor", None, None),
            P("dp", "tensor"),
            P("dp", None, "tensor"),
            P("tensor", "dp"),
            P("dp", "tensor"),
            P("tensor", "dp"),
            P(None, "dp"),
            P(None, "dp"),
            P("tensor", None, None),
        ),
        check_vma=False,
    )
```

```python
import functools

import jax
import jax.numpy as jnp
from jax import lax
from jax.experimental import pallas as pl
from jax.experimental.pallas import tpu as pltpu
from jax.sharding import PartitionSpec as P

HD = 64
GRID = 16
RELS = 2 * GRID - 1
LANES = 128
STRIP = 128

highest = lax.Precision.HIGHEST
epsilon = 1e-06
masked_score = -30000.0
mask_columns = (-29952.0, -48.0)
bf16 = jnp.bfloat16
f32 = jnp.float32
vmem = pltpu.CompilerParams(vmem_limit_bytes=24 * 2**20)


def cast_low(values):
    return values.astype(bf16)


def matmul(left_side, right_side):
    return jnp.dot(left_side, right_side, preferred_element_type=f32)


def matmul_tn(left_side, right_side):
    return lax.dot_general(
        left_side, right_side, (((0,), (0,)), ((), ())), preferred_element_type=f32
    )


def matmul_nt(left_side, right_side):
    return lax.dot_general(
        left_side, right_side, (((1,), (1,)), ((), ())), preferred_element_type=f32
    )


def gelu_pair(hidden):
    cdf = 0.5 + 0.5 * lax.erf(hidden * (0.5**0.5))
    slope = cdf + hidden * jnp.exp(-0.5 * hidden * hidden) * (0.3989422804014327)
    return cast_low(hidden * cdf), cast_low(slope)


def spread_tables(tables):
    n = tables.shape[0]
    lane = jnp.arange(LANES)
    dimension, offset = jnp.divmod(jnp.arange(2 * RELS), RELS)
    own = jnp.arange(GRID)[None, :, None]
    picks = (offset[:, None, None] == own - lane % GRID + GRID - 1) & (
        dimension[:, None, None] == lane // GRID
    )
    parts = matmul(tables, cast_low(picks).reshape(2 * RELS, GRID * LANES))
    parts = jnp.transpose(cast_low(parts).reshape(n, GRID, LANES), (1, 0, 2)).reshape(GRID, -1)
    lane = jnp.tile(lane, n)
    row = jnp.arange(LANES)[:, None]
    ones = cast_low((row == lane) & (row // 2 == GRID))
    parts = [jnp.where(lane // GRID == c, parts, jnp.zeros_like(parts)) for c in range(2)]
    return jnp.pad(jnp.concatenate(parts, axis=0), ((0, LANES - 2 * GRID), (0, 0))) + ones


def table_grad(pairs):
    pairs = pairs[:, : 2 * GRID, : 2 * GRID].reshape(-1, 2, GRID, 2, GRID)
    pairs = jnp.stack([pairs[:, 0, :, 0], pairs[:, 1, :, 1]], axis=1)
    offset = jnp.arange(GRID)[:, None] - jnp.arange(GRID)[None, :] + GRID - 1
    hot = (offset[:, :, None] == jnp.arange(RELS)).astype(f32)
    return jnp.einsum("hcab,abr->hcr", pairs, hot, precision=highest)


def in_hbm(array):
    return pltpu.with_memory_space_constraint(array, pltpu.HBM)


class Projection:
    def __init__(self, views, tile, start, tiles):
        self.views, self.tile, self.start, self.tiles = views, tile, start, tiles

    def arrays(self):
        return [in_hbm(array) for share in self.views for array, _, _ in share]

    def specs(self):
        return [
            pl.BlockSpec((rows, self.tile), lambda t, at=at: (at, self.start + t))
            for share in self.views
            for _, at, rows in share
        ]

    def read(self, refs):
        refs, shares = list(refs), []
        for share in self.views:
            shares.append(joined([refs.pop(0)[...] for _ in share], 0))
        return joined(shares, 1), refs


class BlocksProjection:
    def __init__(self, array, places, tile, start, tiles):
        self.array, self.places, self.tile, self.start, self.tiles = array, places, tile, start, tiles

    def arrays(self):
        return [self.places, in_hbm(self.array)]

    def specs(self):
        return [
            pl.BlockSpec(memory_space=pltpu.SMEM),
            pl.BlockSpec(
                self.array.shape[:2] + (self.tile,), lambda t: (0, 0, self.start + t)
            ),
        ]

    def read(self, refs):
        places, blocks, *refs = refs
        shares, count = self.places.shape
        parts = [[blocks[places[j, r]] for r in range(count)] for j in range(shares)]
        return joined([joined(part, 0) for part in parts], 1), refs


def whole(array):
    return pl.BlockSpec(array.shape, lambda t: (0,) * array.ndim)


def tile_of(array):
    return pl.BlockSpec((None,) + array.shape[1:], lambda t: (t, 0, 0))


def joined(parts, axis):
    return parts[0] if len(parts) == 1 else jnp.concatenate(parts, axis=axis)


def strips(rows):
    return [pl.ds(start, STRIP) for start in range(0, rows, STRIP)]


def project(x, weight, how, slope=None):
    rows, width = x.shape

    def kernel(x_ref, *refs):
        tile, refs = weight.read(refs)
        out = matmul(x_ref[...], tile)
        if how == "gelu":
            refs[0][...], refs[1][...] = gelu_pair(out)
        elif how == "slope":
            refs[1][...] = cast_low(out * refs[0][...].astype(f32))
        else:
            refs[0][...] = cast_low(out)

    result = jax.ShapeDtypeStruct((weight.tiles, rows, width), bf16)
    extra = [] if slope is None else [slope]
    outs = [result] * (2 if how == "gelu" else 1)
    got = pl.pallas_call(
        kernel,
        grid=(weight.tiles,),
        in_specs=[whole(x)] + weight.specs() + [tile_of(e) for e in extra],
        out_specs=[tile_of(out) for out in outs],
        out_shape=outs,
        compiler_params=vmem,
        cost_estimate=pl.CostEstimate(
            flops=2 * rows * width * width * weight.tiles,
            bytes_accessed=2 * width * weight.tiles * (width + 2 * rows),
            transcendentals=0,
        ),
    )(x, *weight.arrays(), *extra)
    return got if how == "gelu" else got[0]


def project_back(h, weight, how, extra=(), params=None, at=()):
    tiles, rows, width = h.shape
    n_extra = len(extra) + (params is not None)

    def kernel(h_ref, *refs):
        tile, refs = weight.read(refs)
        extra, outs, sums = refs[:n_extra], refs[n_extra:-1], refs[-1]
        t = pl.program_id(0)

        def param(i):
            return extra[-1][at[i] : at[i] + 1, :]

        def forward(cut):
            residual = extra[0][cut, :].astype(f32)
            if len(at) > 2:
                residual = residual * param(2) + param(3)
            values = sums[cut, :] + residual
            center = values - jnp.mean(values, axis=-1, keepdims=True)
            scale = lax.rsqrt(jnp.mean(center * center, axis=-1, keepdims=True) + epsilon)
            normed = center * scale
            return normed, scale, cast_low(normed * param(0) + param(1))

        def backward(grad, normed, scale):
            product = grad * normed
            grads = [jnp.sum(product, axis=0, keepdims=True), jnp.sum(grad, axis=0, keepdims=True)]
            scaled = grad * param(0)
            inner = scaled - jnp.mean(scaled, axis=-1, keepdims=True)
            inner = (inner - normed * jnp.mean(scaled * normed, axis=-1, keepdims=True)) * scale
            return inner, cast_low(inner), jnp.concatenate(grads, axis=0)

        total = matmul_nt(h_ref[...], tile)

        @pl.when(t == 0)
        def _():
            sums[...] = total

        @pl.when(t > 0)
        def _():
            sums[...] += total

        @pl.when(t == tiles - 1)
        def _():
            if how == "low":
                for cut in strips(rows):
                    outs[0][cut, :] = cast_low(sums[cut, :])
            elif how == "add":
                for cut in strips(rows):
                    outs[0][cut, :] = cast_low(sums[cut, :] + extra[0][cut, :])
            elif how == "norm":
                for cut in strips(rows):
                    normed, scale, result = forward(cut)
                    outs[0][cut, :] = normed
                    outs[1][cut, :] = scale
                    outs[2][cut, :] = result
                    outs[3][cut, :] = result[:, width // 2 :]
            else:
                param_grads = jnp.zeros((2, width), f32)
                for cut in strips(rows):
                    if how == "final":
                        normed, scale, result = forward(cut)
                        outs[0][cut, :] = result
                        grad = extra[1][cut, :].astype(f32)
                    else:
                        normed, scale = extra[1][cut, :], extra[2][cut, :]
                        grad = sums[cut, :] + extra[0][cut, :]
                    pre, low, strip_grads = backward(grad, normed, scale)
                    param_grads = param_grads + strip_grads
                    outs[-4][cut, :] = pre
                    outs[-3][cut, :] = low
                    outs[-2][cut, :] = low[:, width // 2 :]
                outs[-1][...] = param_grads

    low = jax.ShapeDtypeStruct((rows, width), bf16)
    wide = jax.ShapeDtypeStruct((rows, width), f32)
    part = jax.ShapeDtypeStruct((rows, width // 2), bf16)
    back = [wide, low, part, jax.ShapeDtypeStruct((2, width), f32)]
    outs = {
        "low": [low],
        "add": [low],
        "norm": [wide, jax.ShapeDtypeStruct((rows, 1), f32), low, part],
        "back": back,
        "final": [low] + back,
    }[how]
    extra = list(extra) + ([] if params is None else [params])
    got = pl.pallas_call(
        kernel,
        grid=(tiles,),
        in_specs=[tile_of(h)] + weight.specs() + [whole(e) for e in extra],
        out_specs=[whole(out) for out in outs],
        out_shape=outs,
        scratch_shapes=[pltpu.VMEM((rows, width), f32)],
        compiler_params=vmem,
        cost_estimate=pl.CostEstimate(
            flops=2 * rows * width * width * tiles,
            bytes_accessed=2 * width * tiles * (width + rows) + 12 * rows * width,
            transcendentals=0,
        ),
    )(h, *weight.arrays(), *extra)
    return got if len(outs) > 1 else got[0]


def weight_grad(products, factor, way=None):
    width = products[0][0].shape[1]
    high = width // 2
    rows, columns = high // 2, width // 2
    counts = [product[2].shape[0] for product in products]
    ends = [sum(counts[: i + 1]) for i in range(len(counts))]
    starts = [end - count for end, count in zip(ends, counts)]
    tiles = ends[-1]

    def kernel(*refs):
        sides = [refs[4 * i : 4 * i + 4] for i in range(len(products))]
        outs = refs[4 * len(products) : -len(products)]
        turned = refs[-len(products) :]
        t = pl.program_id(0)
        for (left, left_other, right, right_other), held, start, end in zip(sides, turned, starts, ends):

            @pl.when(t == start)
            def _():
                held[...] = jnp.concatenate([left[...].T, left_other[...].T], axis=1)

            @pl.when((t >= start) & (t < end))
            def _():
                total = matmul(held[...], jnp.concatenate([right[...], right_other[...]], axis=0))
                if factor != 1.0:
                    total = total * factor
                total = cast_low(total)
                if way is None:
                    outs[0][...] = total
                    return
                parts = {
                    (x, y): total[x * rows : (x + 1) * rows, y * columns : (y + 1) * columns]
                    for x in range(2)
                    for y in range(2)
                }
                if way == "both":
                    outs[0][...] = parts[1, 1][: rows // 2]
                    outs[1][...] = parts[1, 1][rows // 2 :]
                    outs[2][...] = parts[1, 0]
                    outs[3][...] = parts[0, 1]
                else:
                    other = (1, 0) if way == "xy" else (0, 1)
                    outs[0][:rows, :] = parts[1, 1]
                    outs[0][rows:, :] = parts[other]
                    outs[1][...] = parts[other[::-1]]
                outs[-1][...] = parts[0, 0]

    def column(rows, columns):
        return pl.BlockSpec((rows, columns), lambda t: (0, t))

    in_specs, args = [], []
    for product, start, count in zip(products, starts, counts):
        depth = product[0].shape[0]
        tile = pl.BlockSpec(
            (None, depth, width),
            lambda t, start=start, count=count: (jnp.clip(t - start, 0, count - 1), 0, 0),
        )
        in_specs += [pl.BlockSpec((depth, high), lambda t: (0, 0))] * 2 + [tile] * 2
        args += product
    if way is None:
        parts = [(high, width)]
    elif way == "both":
        parts = [(rows // 2, columns)] * 2 + [(rows, columns)] * 3
    else:
        parts = [(high, columns), (rows, columns), (rows, columns)]
    outs = pl.pallas_call(
        kernel,
        grid=(tiles,),
        in_specs=in_specs,
        out_specs=[column(*part) for part in parts],
        out_shape=[jax.ShapeDtypeStruct((rows, tiles * columns), bf16) for rows, columns in parts],
        scratch_shapes=[pltpu.VMEM((high, 2 * product[0].shape[0]), bf16) for product in products],
        compiler_params=vmem,
        cost_estimate=pl.CostEstimate(
            flops=sum(4 * high * product[2].size for product in products),
            bytes_accessed=sum(4 * product[2].size + 2 * product[0].size for product in products)
            + 2 * tiles * high * width,
            transcendentals=0,
        ),
    )(*args)
    return outs[0] if way is None else outs


def weight_grad_blocks(products, places):
    rows, width = products[0][0].shape
    shares, count = places.shape
    block, share = width // count, width // shares
    counts = [right.shape[0] for _, right in products]
    ends = [sum(counts[: i + 1]) for i in range(len(counts))]
    starts = [end - count for end, count in zip(ends, counts)]
    tiles = ends[-1]

    def kernel(places, *refs):
        out, turned = refs[2 * len(products)], refs[2 * len(products) + 1 :]
        t = pl.program_id(0)
        for i, (held, start, end) in enumerate(zip(turned, starts, ends)):

            @pl.when(t == start)
            def _():
                held[...] = refs[2 * i][...].T

            @pl.when((t >= start) & (t < end))
            def _():
                total = cast_low(matmul(held[...], refs[2 * i + 1][...]))
                for j in range(shares):
                    for r in range(count):
                        part = total[r * block : (r + 1) * block, j * share : (j + 1) * share]
                        out[places[j, r]] = part

    in_specs, args = [pl.BlockSpec(memory_space=pltpu.SMEM)], [places]
    for (left, right), start, depth in zip(products, starts, counts):
        tile = pl.BlockSpec(
            (None, rows, width),
            lambda t, start=start, depth=depth: (jnp.clip(t - start, 0, depth - 1), 0, 0),
        )
        in_specs += [whole(left), tile]
        args += [left, right]
    return pl.pallas_call(
        kernel,
        grid=(tiles,),
        in_specs=in_specs,
        out_specs=pl.BlockSpec((places.size, block, share), lambda t: (0, 0, t)),
        out_shape=jax.ShapeDtypeStruct((places.size, block, tiles * share), bf16),
        scratch_shapes=[pltpu.VMEM((width, rows), bf16) for _ in products],
        compiler_params=vmem,
        cost_estimate=pl.CostEstimate(
            flops=sum(2 * width * right.size for _, right in products),
            bytes_accessed=sum(2 * right.size for _, right in products) + 2 * tiles * width * width,
            transcendentals=0,
        ),
    )(*args)


def pair_of(array, role):
    return pl.BlockSpec((None, array.shape[1], LANES), lambda i: (role, 0, i))


def attend_forward(q, k, v, hot, spread, other, keep):
    (q, q_role), (k, k_role), (v, v_role) = q, k, v
    spread, first_pair = spread
    rows, n, width = q.shape[1], k.shape[1], q.shape[2]
    heads = width // HD

    def kernel(q_ref, k_ref, v_ref, hot_ref, spread_ref, other_ref, keep_ref, context_ref, probs_ref):
        keys = jnp.concatenate([k_ref[...] * keep_ref[...], other_ref[...]], axis=1)
        values = v_ref[...]
        first = lax.broadcasted_iota(jnp.int32, (rows, LANES), 1) < HD
        queries = q_ref[...] * jnp.asarray(HD**-0.5, bf16)
        parts = []
        for h in range(2):
            mine = jnp.where(first if h == 0 else ~first, queries, jnp.zeros_like(queries))
            bias = cast_low(matmul(hot_ref[...], spread_ref[:, h * LANES : (h + 1) * LANES]))
            scores = matmul_nt(jnp.concatenate([mine, bias], axis=1), keys)
            weights = jnp.exp(scores - jnp.max(scores, axis=1, keepdims=True))
            probs = cast_low(weights * (1.0 / jnp.sum(weights, axis=1, keepdims=True)))
            probs_ref[h] = probs
            parts.append(matmul(probs, values))
        context_ref[...] = cast_low(jnp.where(first, parts[0], parts[1]))

    probs = jax.ShapeDtypeStruct((heads, rows, n), bf16)
    return pl.pallas_call(
        kernel,
        grid=(heads // 2,),
        in_specs=[
            pair_of(q, q_role),
            pair_of(k, k_role),
            pair_of(v, v_role),
            whole(hot),
            pl.BlockSpec((LANES, 2 * LANES), lambda i: (0, first_pair + i)),
            whole(other),
            whole(keep),
        ],
        out_specs=[
            pl.BlockSpec((rows, LANES), lambda i: (0, i)),
            pl.BlockSpec((2, rows, n), lambda i: (i, 0, 0)),
        ],
        out_shape=[jax.ShapeDtypeStruct((rows, width), bf16), probs],
        compiler_params=vmem,
        cost_estimate=pl.CostEstimate(
            flops=8 * heads * rows * n * LANES,
            bytes_accessed=2 * heads * rows * n,
            transcendentals=heads * rows * n,
        ),
    )(q, k, v, hot, spread, other, keep)


def attend_backward(q, k, v, grad, probs, hot, other, keep):
    (q, q_role), (k, k_role), (v, v_role) = q, k, v
    rows, n, width = q.shape[1], k.shape[1], q.shape[2]
    heads = width // HD
    together = q is k

    def kernel(q_ref, k_ref, v_ref, grad_ref, probs_ref, hot_ref, other_ref, keep_ref, *refs):
        if together:
            grads_ref, pairs_ref, held_ref = refs
            dq_ref, dk_ref, dv_ref = (grads_ref.at[i] for i in range(3))
        else:
            dq_ref, dkv_ref, pairs_ref, held_ref = refs
            dk_ref, dv_ref = dkv_ref.at[0], dkv_ref.at[1]
        keep = keep_ref[...]
        keys = jnp.concatenate([k_ref[...] * keep, other_ref[...]], axis=1)
        values = v_ref[...]
        first = lax.broadcasted_iota(jnp.int32, (rows, LANES), 1) < HD
        grad = grad_ref[...]
        turned_queries = q_ref[...].T
        turned_grad = grad.T
        hot = hot_ref[...]
        query_parts, key_parts, value_parts = [], [], []
        for h in range(2):
            mine = jnp.where(first if h == 0 else ~first, grad, jnp.zeros_like(grad))
            prob_grad = matmul_nt(mine, values)
            probs = probs_ref[h].astype(f32)
            mean = jnp.sum(probs * prob_grad, axis=1, keepdims=True)
            held_ref[...] = cast_low(probs * (prob_grad - mean))
            both = matmul(held_ref[...], keys)
            query_parts.append(both[:, :LANES])
            right = both[:, LANES:]
            high = cast_low(right)
            rest = cast_low(right - high.astype(f32))
            pairs_ref[h] = matmul(hot, high) + matmul(hot, rest)
            mine = slice(h * HD, (h + 1) * HD)
            key_parts.append(matmul(turned_queries[mine], held_ref[...]))
            value_parts.append(matmul(turned_grad[mine], probs_ref[h]))
        dq_ref[...] = cast_low(jnp.where(first, query_parts[0], query_parts[1]) * HD**-0.5)
        turned = jnp.concatenate(key_parts, axis=0).T
        dk_ref[...] = cast_low(turned * HD**-0.5 * keep.astype(f32))
        dv_ref[...] = cast_low(jnp.concatenate(value_parts, axis=0).T)

    def grads_of(array):
        return pl.BlockSpec((array.shape[0], array.shape[1], LANES), lambda i: (0, 0, i))

    if together:
        outs = [jax.ShapeDtypeStruct((3, rows, width), bf16)]
    else:
        outs = [jax.ShapeDtypeStruct((1, rows, width), bf16), jax.ShapeDtypeStruct((2, n, width), bf16)]
    out_specs = [grads_of(out) for out in outs]
    if not together:
        out_specs[0] = pl.BlockSpec((None, rows, LANES), lambda i: (0, 0, i))
    outs.append(jax.ShapeDtypeStruct((heads, LANES, LANES), f32))
    out_specs.append(pl.BlockSpec((2, LANES, LANES), lambda i: (i, 0, 0)))
    return pl.pallas_call(
        kernel,
        grid=(heads // 2,),
        in_specs=[
            pair_of(q, q_role),
            pair_of(k, k_role),
            pair_of(v, v_role),
            pl.BlockSpec((rows, LANES), lambda i: (0, i)),
            pl.BlockSpec((2, rows, n), lambda i: (i, 0, 0)),
            whole(hot),
            whole(other),
            whole(keep),
        ],
        out_specs=out_specs,
        out_shape=outs,
        scratch_shapes=[pltpu.VMEM((rows, n), bf16)],
        compiler_params=vmem,
        cost_estimate=pl.CostEstimate(
            flops=20 * heads * rows * n * LANES, bytes_accessed=2 * heads * rows * n, transcendentals=0
        ),
    )(q, k, v, grad, probs, hot, other, keep)


GATHERS = (
    (("qkv",), "both"),
    (("outa", "ina",), "both"),
    (("mlpa",), "both"),
    (("q", "kv", "outb", "inb", "mlpb",), "blocks"),
)
SCATTERS = (
    (("mlpb", "inb",), "blocks"),
    (("q", "kv", "outb", "mlpa",), "both"),
    (("ina", "outa",), "both"),
    (("qkv",), "both"),
)

PAGE, LAYERS, OUT, VISION, TEXT, SMALL, W1, W2, W3, W4, G1, G2, G3, G4 = range(1, 15)
GATHER, SCATTER = W1, G1

ORDER = (
    W1, PAGE, W1, W1, PAGE, W2, W2, W1, PAGE, W3, W1, W2, PAGE, W1, PAGE, LAYERS, LAYERS, W3,
    LAYERS, W2, W3, W2, W2, LAYERS, LAYERS, W3, W3, W3, LAYERS, W4, LAYERS, LAYERS, LAYERS,
    LAYERS, LAYERS, LAYERS, LAYERS, -G1, OUT, -G2, LAYERS, G2, LAYERS, LAYERS, VISION, -G2, G2,
    LAYERS, -G3, G3, -G4, G4, G2, LAYERS, -G3, G3, G2, LAYERS, -G4, G3, G2, TEXT, G4, G3, SMALL,
    SMALL, G2, G4, SMALL, G3, SMALL, G4, SMALL, G3, G4, SMALL, G4, G1,
)


class Flows:
    def __init__(self, token):
        self.token = token
        self.flows, self.pending, self.results = {}, {}, {}

    def add(self, name, flow):
        self.flows[name] = flow
        self.pending[name] = next(flow)

    def step(self, *names):
        held = [self.pending[name] for name in names]
        held, self.token = lax.optimization_barrier((held, self.token))
        for name, arrays in zip(names, held):
            self.send(name, arrays)

    def mark(self, values):
        values, self.token = lax.optimization_barrier((values, self.token))
        return values

    def send(self, name, arrays):
        try:
            arrays = self.flows[name].send(arrays)
            self.pending[name] = self.mark(arrays) if name == LAYERS else arrays
        except StopIteration as end:
            self.results[name] = end.value


def shards(
    text_rows,
    vision_rows,
    segment_ids,
    text_keep,
    segment_box,
    patch_keep,
    attn_qkv_a,
    attn_out_a,
    mlp_in_a,
    mlp_out_a,
    norm_gain_a,
    norm_shift_a,
    box_table_a,
    attn_query_b,
    attn_kv_b,
    attn_out_b,
    mlp_in_b,
    mlp_out_b,
    norm_gain_b,
    norm_shift_b,
    box_table_b,
    out_grad,
):
    pages, length, width = text_rows.shape
    patches = vision_rows.shape[1]
    ndp, nt = lax.axis_size("dp"), lax.axis_size("tensor")
    own, mine = lax.axis_index("dp"), lax.axis_index("tensor")
    block = width // ndp
    share = attn_out_a.shape[0]
    tiles = mlp_in_a.shape[1] // share
    nz = ndp // 4
    z_bits = [range(3, ndp.bit_length() - 1), range(2, 3)]
    copies = nt // pages
    direct = nt == 2 and share % LANES == 0

    def swap(values, dp_mask, tensor_mask):
        pairs = [
            (d * nt + t, (d ^ dp_mask) * nt + (t ^ tensor_mask))
            for d in range(ndp)
            for t in range(nt)
        ]
        return lax.ppermute(flows.mark(values), ("dp", "tensor"), pairs)

    def in_order(relative):
        return [
            lax.select_n(mine, *[relative[a ^ m] for m in range(nt)])
            for a in range(nt)
        ]

    def gather_rows(piece, way):
        (piece,) = yield [piece]
        for bits in z_bits:
            for bit in reversed(bits):
                others = [swap(piece, 1 << bit, 0)]
                if bit == bits[0]:
                    others = yield others
                piece = jnp.concatenate([piece, *others], axis=0)
        rows = piece.shape[0]
        half = rows // 2

        if direct and way == "both":
            along_x, along_y = yield swap(piece, 2, 0), swap(piece, 0, 1)
            first = (piece, along_x, along_y)
            *far, piece_c, along_x_c, along_y_c = yield (
                swap(along_y[:half], 2, 0),
                swap(along_x[half:], 0, 1),
                *[swap(array, 1, 0) for array in first],
            )
            far_c = yield [swap(array, 1, 0) for array in far]
            return [
                [(array, 0, rows) for array in (piece, along_x, piece_c, along_x_c)],
                [(along_y, 0, rows)]
                + [(array, 0, half) for array in far]
                + [(along_y_c, 0, rows)]
                + [(array, 0, half) for array in far_c],
            ]
        if direct and way == "yx":
            (along_y,) = yield [swap(piece, 0, 1)]
            near = jnp.concatenate([piece, along_y], axis=0)
            far, near_c = yield swap(near, 2, 0), swap(near, 1, 0)
            (far_c,) = yield [swap(far, 1, 0)]
            return [[(array, j, rows) for array in (near, far, near_c, far_c)] for j in range(2)]
        (along_x,) = yield [swap(piece, 2, 0)]
        near = jnp.concatenate([piece, along_x], axis=0)
        near_c, *others = yield [swap(near, 1, 0)] + [swap(near, 0, j) for j in range(1, nt)]
        others_c = yield [swap(array, 1, 0) for array in others]
        return [
            [(array, 0, 2 * rows), (array_c, 0, 2 * rows)]
            for array, array_c in zip([near, *others], [near_c, *others_c])
        ]

    def projection(*names):
        group = next(group for group in gathers if names[0] in group)
        views = results[gathers[group]]
        counts = [pieces[name].shape[1] // share for name in group]
        first = group.index(names[0])
        start, tiles = sum(counts[:first]), sum(counts[first : first + len(names)])
        if not isinstance(views, list):
            return BlocksProjection(views, places, share, start, tiles)
        if direct:
            return Projection(views, share, start, tiles)
        shares = [
            jnp.concatenate([array[:, start * share : (start + tiles) * share] for array, _, _ in part], axis=0)
            for part in views
        ]
        both = jnp.stack([part.reshape(width, tiles, share) for part in shares], axis=2)
        return Projection([[(both.reshape(width, tiles * width), 0, width)]], width, 0, tiles)

    def at_once(flow, arrays):
        try:
            while True:
                arrays = flow.send(arrays)
        except StopIteration as end:
            return end.value

    def gather_blocks(piece):
        if direct:
            (blocks,) = yield [lax.all_gather(flows.mark(piece), ("dp", "tensor"))]
            return blocks
        (piece,) = yield [piece]
        flow = gather_rows(piece, "xy")
        return at_once(flow, next(flow))

    def scatter_blocks(names):
        sides = yield
        if direct:
            held = {key: array for key, (array, _) in sides.items()}
            products = [(held[name, "left"], held[name, "right"]) for name in names]
            parts = weight_grad_blocks(products, places)
            parts = flows.mark(parts.reshape(-1, parts.shape[2]))
            (out,) = yield [
                lax.psum_scatter(parts, ("dp", "tensor"), scatter_dimension=0, tiled=True)
            ]
            return out
        yield []
        flow = scatter_rows(names, "xy")
        next(flow)
        flow.send(flow.send(sides))
        return at_once(flow, {})

    def scatter_rows(names, way):
        held, others = {}, {}
        for _ in range(2):
            given = yield
            held.update({key: array for key, (array, _) in given.items()})
            got = yield [swap(part, 1, 0) for _, part in given.values()]
            others.update(zip(given, got))
        products = [
            tuple(found[name, side] for side in ("left", "right") for found in (held, others))
            for name in names
        ]
        rows = width // 4
        half = rows // 2
        if direct:
            away, *near, here = weight_grad(products, 1.0 / copies, way)
            if way == "both":
                far_y, near_x, near_y = near
                from_x, from_y = yield swap(away, 2, 0), swap(far_y, 0, 1)
                near_y = lax.dynamic_update_slice(near_y, near_y[:half] + from_x, (0, 0))
                near_x = lax.dynamic_update_slice(near_x, near_x[half:] + from_y, (half, 0))
                got = yield swap(near_x, 2, 0), swap(near_y, 0, 1)
            else:
                masks = ((2, 0), (0, 1)) if way == "xy" else ((0, 1), (2, 0))
                (came,) = yield [swap(away, *masks[0])]
                (other,) = yield [swap(near[0] + came[:rows], *masks[1])]
                got = [came[rows:], other]
        else:
            total = weight_grad(products, 1.0 / copies).reshape(2, rows, -1, nt, share)
            parts = [[total[x, :, :, j].reshape(rows, -1) for j in range(nt)] for x in range(2)]
            from_x = yield [swap(part, 2, 0) for part in parts[1]]
            near = [part + came for part, came in zip(parts[0], from_x)]
            here = near[0]
            got = yield [swap(near[j], 0, j) for j in range(1, nt)]
        for bits in reversed(z_bits):
            for bit in bits:
                half = here.shape[0] // 2
                away = sum([part[half:] for part in got], here[half:].astype(f32))
                here = sum([part[:half] for part in got], here[:half].astype(f32))
                got = [swap(cast_low(away), 1 << bit, 0)]
                if bit == bits[-1]:
                    got = yield got
        return here + got[0]

    def to_owners(rows):
        cut = rows.shape[0] // nt
        parts = [rows[a * cut : (a + 1) * cut] for a in range(nt)]
        relative = in_order(parts)
        arrived = yield [relative[0]] + [swap(relative[k], 0, k) for k in range(1, nt)]
        return jnp.stack(in_order(arrived)[::copies])

    def page_parts():
        (rows_text, rows_vision, shares, ids, box, kept_text, kept_patch) = yield [
            text_rows, vision_rows, out_grad, segment_ids, segment_box, text_keep, patch_keep
        ]
        feature = source * block + jnp.arange(width) % block
        order = cast_low(jnp.arange(width)[:, None] == feature[None, :])
        shares = in_order([shares[a // copies] for a in range(nt)])
        tables = jnp.stack([box_table_a, box_table_b])
        got = yield [
            order,
            [swap(tables, 0, j) for j in range(1, nt)],
            [swap(shares[j], 0, j) for j in range(1, nt)],
        ]
        order, other_tables, other_shares = got
        page = mine // copies

        def of_page(values):
            return lax.dynamic_index_in_dim(values, page, 0, keepdims=False)

        text = cast_low(matmul(of_page(rows_text), order))
        vision = cast_low(matmul(of_page(rows_vision), order))
        text, vision = yield text, vision

        lane = jnp.arange(LANES)
        target = jnp.where(lane < 2 * GRID, lane % GRID, 1)
        select = jnp.stack([lane // GRID == 0, lane // GRID == 1]).astype(f32)
        fill = (lane // 2 == GRID).astype(f32)
        segment_hot = (of_page(ids)[:, None] == jnp.arange(box.shape[1])).astype(f32)
        token_box = matmul(segment_hot, matmul(of_page(box).astype(f32), select) + fill)
        hot = cast_low(token_box == target)
        patch = jnp.arange(patches)[:, None]
        patch_box = jnp.where(lane // GRID == 0, patch % GRID, patch // GRID)
        patch_box = jnp.where(lane < 2 * GRID, patch_box, fill.astype(jnp.int32))
        patch_hot = cast_low(patch_box == target)

        def other_columns(hot, keep):
            kept = (keep > 0).astype(bf16)[:, None]
            score = jnp.where(lane == 2 * GRID, *[jnp.asarray(m, bf16) for m in mask_columns])
            other = hot * jnp.where(lane < 2 * GRID, kept, score * (1 - kept))
            return other, jnp.broadcast_to(kept, other.shape)

        other_a = other_columns(hot, of_page(kept_text))
        other_b = other_columns(patch_hot, of_page(kept_patch))
        tables = jnp.concatenate([tables] + other_tables, axis=1)
        spread = spread_tables(tables.reshape(-1, 2 * RELS))
        hot, turned, other_a, other_b, spread = yield hot, hot.T, other_a, other_b, spread
        grad_in = jnp.concatenate(in_order([shares[0]] + other_shares), axis=0)
        (grad_in,) = yield [cast_low(matmul(grad_in, order))]
        return order, text, vision, grad_in, hot, turned, other_a, other_b, spread

    at = jnp.arange(width) // block
    relative = at // (2 * nz) + 2 * (at // nz % 2)
    for bit in range(2, ndp.bit_length() - 1):
        relative = relative + (1 << bit) * (at // (nz >> (bit - 1)) % 2)
    source = own ^ relative
    places = source[::block] * nt + (mine ^ jnp.arange(nt, dtype=jnp.int32))[:, None]

    flows = Flows(text_keep[0, 0])

    norms = jnp.concatenate([norm_gain_a, norm_shift_a, norm_gain_b, norm_shift_b], axis=0)
    norm_columns = jnp.pad(norms.T, ((0, 0), (0, LANES - norms.shape[0])))
    def weights(*pieces):
        return gather_rows(jnp.concatenate(pieces, axis=1))

    pieces = {
        "qkv": attn_qkv_a.reshape(block, -1),
        "outa": attn_out_a.T,
        "ina": mlp_in_a,
        "mlpa": mlp_out_a.T,
        "q": attn_query_b,
        "kv": attn_kv_b.reshape(block, -1),
        "outb": attn_out_b.T,
        "inb": mlp_in_b,
        "mlpb": mlp_out_b.T,
    }
    gathers, scatters = {}, {}
    for i, (group, way) in enumerate(GATHERS):
        gathers[group] = GATHER + i
        own_pieces = [pieces[name] for name in group] + [norm_columns] * ("qkv" in group)
        piece = jnp.concatenate(own_pieces, axis=1)
        gather = gather_blocks(piece) if way == "blocks" else gather_rows(piece, way)
        flows.add(gathers[group], gather)
    flows.add(PAGE, page_parts())
    for i, (group, way) in enumerate(SCATTERS):
        scatters[group] = SCATTER + i
        scatter = scatter_blocks(group) if way == "blocks" else scatter_rows(group, way)
        flows.add(scatters[group], scatter)
    results = flows.results
    sides, sent = {}, set()
    tables_grads, norm_grads = {}, {}
    high = width // 2

    def given(flow):
        group = next(group for group, name in scatters.items() if name == flow)
        ready = {key: side for key, side in sides.items() if key[0] in group and key not in sent}
        sent.update(ready)
        return ready

    def chain():
        yield []
        order, text, vision, grad_in, hot, turned, other_a, other_b, spread = results[PAGE]
        pairs = spread.shape[1] // (4 * LANES)
        sides["kv", "left"] = (vision, vision[:, high:])
        sides["qkv", "left"] = (text, text[:, high:])

        group = next(group for group in gathers if "qkv" in group)
        at = sum(pieces[name].shape[1] for name in group)
        norms = [
            array[i * rows : (i + 1) * rows, at : at + 8]
            for array, i, rows in results[gathers[group]][0]
        ]
        (norms,) = yield [jnp.concatenate(norms, axis=0).T.astype(f32)]
        qkv_a = projection("qkv")
        (qkv,) = yield [project(text, qkv_a, "low")]
        triple_a = ((qkv, 0), (qkv, 1), (qkv, 2))
        context_a, probs_a = yield attend_forward(*triple_a, hot, (spread, 0), *other_a)
        out_a = projection("outa")
        normed_a0, scale_a0, mixed_a, part = yield project_back(
            context_a[None], out_a, "norm", [text], norms, (0, 2)
        )
        sides["outa", "right"] = (context_a[None], context_a[None])
        sides["ina", "left"] = (mixed_a, part)
        in_a = projection("ina")
        gelu_a, slope_a = yield project(mixed_a, in_a, "gelu")
        sides["mlpa", "right"] = (gelu_a, gelu_a)
        back_a = projection("mlpa")
        normed_a1, scale_a1, middle, part = yield project_back(
            gelu_a, back_a, "norm", [normed_a0], norms, (1, 3, 0, 2)
        )
        sides["q", "left"] = (middle, part)

        query_b, kv_b = projection("q"), projection("kv")
        queries_b, kv = yield project(middle, query_b, "low"), project(vision, kv_b, "low")
        triple_b = ((queries_b, 0), (kv, 0), (kv, 1))
        context_b, probs_b = yield attend_forward(*triple_b, hot, (spread, pairs), *other_b)
        out_b = projection("outb")
        normed_b0, scale_b0, mixed_b, part = yield project_back(
            context_b[None], out_b, "norm", [normed_a1], norms, (4, 6, 1, 3)
        )
        sides["outb", "right"] = (context_b[None], context_b[None])
        sides["inb", "left"] = (mixed_b, part)
        in_b = projection("inb")
        gelu_b, slope_b = yield project(mixed_b, in_b, "gelu")
        sides["mlpb", "right"] = (gelu_b, gelu_b)
        back_b = projection("mlpb")
        final, pre, branch, part, norm_grads["b1"] = yield project_back(
            gelu_b, back_b, "final", [normed_b0, grad_in], norms, (5, 7, 4, 6)
        )

        sides["mlpb", "left"] = (branch, part)
        flows.add(OUT, to_owners(cast_low(matmul_nt(final, order))))
        (hidden,) = yield [project(branch, back_b, "slope", slope_b)]
        sides["inb", "right"] = (hidden, hidden)
        pre, attn_grad, part, norm_grads["b0"] = project_back(
            hidden, in_b, "back", [pre, normed_b0, scale_b0], norms, (4,)
        )
        (context_grad,) = project(attn_grad, out_b, "low")
        pre, attn_grad, part, context_grad = yield pre, attn_grad, part, context_grad
        sides["outb", "left"] = (attn_grad, part)
        query_grad, kv_grad, tables_grads["b"] = yield attend_backward(
            *triple_b, context_grad, probs_b, turned, *other_b
        )
        sides["q", "right"] = (query_grad, query_grad)
        sides["kv", "right"] = (kv_grad, kv_grad)
        vision_grad = project_back(kv_grad, kv_b, "low")
        flows.add(VISION, to_owners(cast_low(matmul_nt(vision_grad, order))))
        pre, branch, part, norm_grads["a1"] = yield project_back(
            query_grad, query_b, "back", [pre, normed_a1, scale_a1], norms, (1,)
        )
        sides["mlpa", "left"] = (branch, part)
        (hidden,) = yield [project(branch, back_a, "slope", slope_a)]
        sides["ina", "right"] = (hidden, hidden)
        pre, attn_grad, part, norm_grads["a0"] = project_back(
            hidden, in_a, "back", [pre, normed_a0, scale_a0], norms, (0,)
        )
        (context_grad,) = project(attn_grad, out_a, "low")
        pre, attn_grad, part, context_grad = yield pre, attn_grad, part, context_grad
        sides["outa", "left"] = (attn_grad, part)
        qkv_grad, tables_grads["a"] = yield attend_backward(
            *triple_a, context_grad, probs_a, turned, *other_a
        )
        sides["qkv", "right"] = (qkv_grad, qkv_grad)
        text_grad = project_back(qkv_grad, qkv_a, "add", [pre])
        flows.add(TEXT, to_owners(cast_low(matmul_nt(text_grad, order))))
        flows.add(SMALL, small_sums(order))

    def small_sums(order):
        norms = jnp.concatenate([norm_grads[i] for i in ("a0", "a1", "b0", "b1")], axis=0)
        norms = lax.dot_general(
            norms, order.astype(f32), (((1,), (1,)), ((), ())), precision=highest, preferred_element_type=f32
        )
        tables = jnp.stack([table_grad(tables_grads["a"]), table_grad(tables_grads["b"])])
        kept = (2, tables.shape[1] // nt, 2, RELS)
        tables = tables.reshape(2, nt, -1)
        size = 2 * tables.shape[2]
        tables = jnp.stack(in_order([tables[:, j].reshape(size) for j in range(nt)]))
        total = jnp.concatenate([norms, jnp.pad(tables, ((0, 0), (0, width - size)))], axis=0)
        (total,) = yield [total * (1.0 / copies)]
        for bits in (range(1), range(1, 2), *z_bits):
            for bit in bits:
                got = [swap(total, 1 << bit, 0)]
                if bit == bits[-1]:
                    got = yield got
                total = total + got[0]
        got = yield [swap(total, 0, j) for j in range(1, nt)]
        total = sum(got, total)
        norms = lax.dynamic_slice(total, (0, own * block), (8, block))
        tables = lax.dynamic_slice(total, (8 + mine, 0), (1, size))
        return norms, tables.reshape(kept)

    flows.add(LAYERS, chain())
    for name in ORDER:
        if name < 0:
            flows.send(-name, given(-name))
        else:
            flows.step(name)
    norm_sums, tables = results[SMALL]
    tables = tables + (flows.token - text_keep[0, 0]).astype(f32)
    grads = {}
    for group, flow in scatters.items():
        start = 0
        for name in group:
            size = pieces[name].shape[1]
            grads[name] = results[flow][:, start : start + size].astype(f32)
            start += size

    return (
        results[OUT],
        results[TEXT].astype(f32),
        results[VISION].astype(f32),
        grads["qkv"].reshape(block, 3, share),
        grads["outa"].T,
        grads["ina"],
        grads["mlpa"].T,
        norm_sums[0:4:2],
        norm_sums[1:4:2],
        tables[0],
        grads["q"],
        grads["kv"].reshape(block, 2, share),
        grads["outb"].T,
        grads["inb"],
        grads["mlpb"].T,
        norm_sums[4:8:2],
        norm_sums[5:8:2],
        tables[1],
    )


def solution(mesh):
    return jax.shard_map(
        shards,
        mesh=mesh,
        in_specs=(
            P("dp", None, None),
            P("dp", None, None),
            P("dp", None),
            P("dp", None),
            P("dp", None, None),
            P("dp", None),
            P("dp", None, "tensor"),
            P("tensor", "dp"),
            P("dp", "tensor"),
            P("tensor", "dp"),
            P(None, "dp"),
            P(None, "dp"),
            P("tensor", None, None),
            P("dp", "tensor"),
            P("dp", None, "tensor"),
            P("tensor", "dp"),
            P("dp", "tensor"),
            P("tensor", "dp"),
            P(None, "dp"),
            P(None, "dp"),
            P("tensor", None, None),
            P("dp", "tensor", None),
        ),
        out_specs=(
            P("dp", "tensor", None),
            P("dp", "tensor", None),
            P("dp", "tensor", None),
            P("dp", None, "tensor"),
            P("tensor", "dp"),
            P("dp", "tensor"),
            P("tensor", "dp"),
            P(None, "dp"),
            P(None, "dp"),
            P("tensor", None, None),
            P("dp", "tensor"),
            P("dp", None, "tensor"),
            P("tensor", "dp"),
            P("dp", "tensor"),
            P("tensor", "dp"),
            P(None, "dp"),
            P(None, "dp"),
            P("tensor", None, None),
        ),
        check_vma=False,
    )
```
